32 devices in a mesh: row: 8 (over z, core), col: 4 (over y, x).
Axes of the slice: x: 2, y: 2, z: 4, core: 2. Of those that a mesh axis runs over, the one named last changes fastest.
Arguments:
- factor_a: bfloat16 [16384, 1024], P(('col', 'row')), may hold values from -0.1875 to 0.1875
- factor_b: bfloat16 [16384, 1024], P(('col', 'row')), may hold values from -0.1875 to 0.1875
- factor_c: bfloat16 [16384, 1024], P(('col', 'row')), may hold values from -0.1875 to 0.1875
Outputs:
- grad_a: float32 [16384, 1024], P(('col', 'row'))
- grad_b: float32 [16384, 1024], P(('col', 'row'))
- grad_c: float32 [16384, 1024], P(('col', 'row'))
The draws below stay inside these ranges and needn't reach their ends.
All inputs are finite; a program needn't handle non-finite values.
Results may differ from the reference program's by a relative error of at most 0.0095.
Values may be sent and summed in bfloat16 or wider, within the bound.
No kernel may reach another device: no remote copies, remote signals or barrier semaphores. Data moves between devices by JAX's collectives and lax.ppermute only.
A program may use at most 192 MiB of HBM per device.

```python
import jax
import jax.numpy as jnp
from jax import lax

NMAT = 32
RANK = 16384
FT = 1024
N_COL = 4


def level_of(rng, shape, cuts, low, top_value):
    level = 1.0
    for position, shards_of in cuts:
        steps = jax.random.uniform(jax.random.fold_in(jax.random.fold_in(rng, 6), position), (shards_of,), jnp.float32, low / len(cuts), top_value / len(cuts))
        level = level * jnp.repeat(jnp.exp(steps), shape[position] // shards_of).reshape((-1,) + (1,) * (len(shape) - 1 - position))
    return level


def scatter_about(key, dims, scale, reach, split=(), kind=jnp.bfloat16):
    entries = scale * jax.random.normal(key, dims, jnp.float32)
    if split:
        entries = entries * level_of(key, dims, split, -0.22, 0.18)
    return jnp.clip(entries, -reach, reach).astype(kind)


def setup_inputs(seed: int = 0) -> dict:
    arg_keys = jax.random.split(jax.random.key(seed), 4)
    factor_a = scatter_about(arg_keys[0], (RANK, FT), FT ** -0.5, 0.1875, ((0, 32),))
    factor_b = scatter_about(arg_keys[1], (RANK, FT), FT ** -0.5, 0.1875, ((0, 32),))
    factor_c = scatter_about(arg_keys[2], (RANK, FT), FT ** -0.5, 0.1875, ((0, 32),))
    return dict(factor_a=factor_a, factor_b=factor_b, factor_c=factor_c)


def reference(factor_a, factor_b, factor_c):
    width = RANK // N_COL
    factors = (factor_a, factor_b, factor_c)

    def one_block(carry, index):
        start = (index * width).astype(jnp.int32)
        pieces = [lax.dynamic_slice_in_dim(f, start, width, 0) for f in factors]
        grams = [lax.dot_general(p, f, (((1,), (1,)), ((), ())), preferred_element_type=jnp.float32) for p, f in zip(pieces, factors)]
        hadam_a = (grams[1] * grams[2]).astype(jnp.bfloat16)
        hadam_b = (grams[2] * grams[0]).astype(jnp.bfloat16)
        hadam_c = (grams[0] * grams[1]).astype(jnp.bfloat16)
        hadams = (hadam_a, hadam_b, hadam_c)
        parts = [lax.dot_general(h, p, (((0,), (0,)), ((), ())), preferred_element_type=jnp.float32).astype(jnp.bfloat16) for p, h in zip(pieces, hadams)]
        new_carry = tuple(c + q.astype(jnp.float32) for c, q in zip(carry, parts))
        return new_carry, None

    zeros = jnp.zeros((RANK, FT), jnp.float32)
    summed, _ = lax.scan(one_block, (zeros, zeros, zeros), jnp.arange(N_COL, dtype=jnp.int32))
    cube_a = factor_a.astype(jnp.float32).reshape(RANK, NMAT, NMAT)
    cube_b = factor_b.astype(jnp.float32).reshape(RANK, NMAT, NMAT)
    cube_c = factor_c.astype(jnp.float32).reshape(RANK, NMAT, NMAT)
    data_a = jnp.einsum('rjk,rki->rij', cube_b, cube_c).reshape(RANK, FT)
    data_b = jnp.einsum('rki,rij->rjk', cube_c, cube_a).reshape(RANK, FT)
    data_c = jnp.einsum('rij,rjk->rki', cube_a, cube_b).reshape(RANK, FT)
    grad_a = NMAT * (summed[0] - data_a)
    grad_b = NMAT * (summed[1] - data_b)
    grad_c = NMAT * (summed[2] - data_c)
    return (grad_a, grad_b, grad_c)
```

```python
import functools

import jax
import jax.numpy as jnp
from jax import lax
from jax.experimental import pallas as pl
from jax.experimental.pallas import tpu as pltpu
from jax.sharding import PartitionSpec as P

NMAT = 32
ROW_TILE = 256
LANES = 128
VMEM_BYTES = 60 * 1024 * 1024


def trace_kernel(feat, x_ref, out_ref, left, right, prod):
    blocks = [slice(f * feat, (f + 1) * feat) for f in range(3)]
    for out, (l, r) in enumerate(((1, 2), (2, 0), (0, 1))):
        left[...] = x_ref[:, blocks[l]].astype(jnp.float32).T
        right[...] = x_ref[:, blocks[r]].astype(jnp.float32).T

        def rows(step, carry):
            base = step * 4
            sums = [None] * 4
            for k in range(NMAT):
                line = right[k * NMAT : (k + 1) * NMAT, :]
                for n in range(4):
                    term = left[pl.ds((base + n) * NMAT + k, 1), :] * line
                    sums[n] = term if k == 0 else sums[n] + term
            for n in range(4):
                prod[pl.ds(base + n, NMAT, stride=NMAT), :] = sums[n]
            return carry

        lax.fori_loop(0, NMAT // 4, rows, 0)
        out_ref[:, blocks[out]] = -prod[...].T


def trace_terms(x):
    rows, width = x.shape
    feat = width // 3
    spec = pl.BlockSpec((LANES, width), lambda i: (i, 0))
    return pl.pallas_call(
        functools.partial(trace_kernel, feat),
        grid=(rows // LANES,),
        in_specs=[spec],
        out_specs=spec,
        out_shape=jax.ShapeDtypeStruct((rows, width), jnp.float32),
        scratch_shapes=[pltpu.VMEM((feat, LANES), jnp.float32)] * 3,
        compiler_params=pltpu.CompilerParams(vmem_limit_bytes=VMEM_BYTES),
        cost_estimate=pl.CostEstimate(flops=rows * feat * NMAT * 6 * 200, bytes_accessed=rows * width * 6, transcendentals=0),
    )(x)


def pair_kernel(feat, i_rows, spans, tile, n_sums, narrow, has_y, *refs):
    refs = list(refs)
    take = lambda n: [refs.pop(0) for _ in range(n)]
    tiles = sum(count for _, count in spans) // tile
    n_i = sum(i_rows) // ROW_TILE
    per = n_i // n_sums
    blocks = [slice(f * feat, (f + 1) * feat) for f in range(3)]
    i_refs, j_refs = take(len(i_rows)), take(len(spans))
    y_refs = take(n_sums) if has_y else []
    out_refs = take(n_i if narrow else n_sums)
    ibuf, jbuf, acc, i_sem, j_sem, y_sem, o_sem = take(7)
    packed = take(1)[0] if narrow else None

    def block(i):
        return pl.ds(i * ROW_TILE, ROW_TILE)

    def fill(buf, sem, sources, ranges, t, size):
        low = 0
        for ref, (first, count) in zip(sources, ranges):
            a, b = max(low, t * size), min(low + count, (t + 1) * size)
            if a < b:
                src = ref.at[pl.ds(first + a - low, b - a)]
                pltpu.make_async_copy(src, buf.at[pl.ds(a, b - a)], sem.at[t]).start()
            low += count

    fill(jbuf, j_sem, j_refs, spans, 0, tile)
    for i in range(n_i):
        fill(ibuf, i_sem, i_refs, [(0, count) for count in i_rows], i, ROW_TILE)
        if has_y:
            pltpu.make_async_copy(y_refs[i // per].at[block(i % per)], acc.at[block(i)], y_sem.at[i]).start()
    for t in range(1, tiles):
        fill(jbuf, j_sem, j_refs, spans, t, tile)

    def wait(ref, sem):
        pltpu.make_async_copy(ref, ref, sem).wait()

    def over_tiles(t, carry):
        cols = pl.ds(pl.multiple_of(t * tile, tile), tile)
        wait(jbuf.at[cols], j_sem.at[t])

        def over_rows(i, inner):
            span = pl.ds(pl.multiple_of(i * ROW_TILE, ROW_TILE), ROW_TILE)

            @pl.when(t == 0)
            def _():
                wait(ibuf.at[span], i_sem.at[i])

            grams = [
                lax.dot_general(ibuf[span, b], jbuf[cols, b], (((1,), (1,)), ((), ())), preferred_element_type=jnp.float32)
                for b in blocks
            ]
            hadams = [(grams[(f + 1) % 3] * grams[(f + 2) % 3]).astype(jnp.bfloat16) for f in range(3)]

            @pl.when(t == 0)
            def _():
                if has_y:
                    wait(acc.at[span], y_sem.at[i])
                else:
                    acc[span, :] = jnp.zeros((ROW_TILE, 3 * feat), jnp.float32)

            for hadam, b in zip(hadams, blocks):
                acc[span, b] += jnp.dot(hadam, jbuf[cols, b], preferred_element_type=jnp.float32)

            @pl.when(t == tiles - 1)
            def _():
                for n in range(n_i):
                    @pl.when(i == n)
                    def _():
                        if narrow:
                            packed[block(n), :] = acc[block(n), :].astype(jnp.bfloat16)
                            src, dst = packed.at[block(n)], out_refs[n]
                        else:
                            src, dst = acc.at[block(n)], out_refs[n // per].at[block(n % per)]
                        pltpu.make_async_copy(src, dst, o_sem.at[n]).start()
            return inner

        return lax.fori_loop(0, n_i, over_rows, carry)

    lax.fori_loop(0, tiles, over_tiles, 0)
    for i in range(n_i):
        wait((packed if narrow else acc).at[block(i)], o_sem.at[i])


def pair_sums(lefts, rights, sums, tile, narrow=False):
    width = lefts[0].shape[1]
    feat = width // 3
    i_rows = [v.shape[0] for v in lefts]
    rows = sum(i_rows)
    rights = [r if isinstance(r, tuple) else (r, 0, r.shape[0]) for r in rights]
    spans = [(first, count) for _, first, count in rights]
    total = sum(count for _, count in spans)
    assert total % tile == 0 and rows % ROW_TILE == 0
    n_i = rows // ROW_TILE
    has_y = sums is not None
    n_sums = len(sums) if has_y else 1
    any_spec = pl.BlockSpec(memory_space=pl.ANY)
    operands = [*lefts, *(r for r, _, _ in rights), *(sums or [])]
    first_y = len(lefts) + len(rights)
    if narrow:
        outs = [jax.ShapeDtypeStruct((ROW_TILE, width), jnp.bfloat16)] * n_i
    else:
        outs = [jax.ShapeDtypeStruct((rows // n_sums, width), jnp.float32)] * n_sums
    scratch = [
        pltpu.VMEM((rows, width), jnp.bfloat16),
        pltpu.VMEM((total, width), jnp.bfloat16),
        pltpu.VMEM((rows, width), jnp.float32),
        pltpu.SemaphoreType.DMA((n_i,)),
        pltpu.SemaphoreType.DMA((total // tile,)),
        pltpu.SemaphoreType.DMA((n_i,)),
        pltpu.SemaphoreType.DMA((n_i,)),
    ]
    if narrow:
        scratch.append(pltpu.VMEM((rows, width), jnp.bfloat16))
    return pl.pallas_call(
        functools.partial(pair_kernel, feat, i_rows, spans, tile, n_sums, narrow, has_y),
        in_specs=[any_spec] * len(operands),
        out_specs=[any_spec] * len(outs),
        out_shape=outs,
        scratch_shapes=scratch,
        input_output_aliases={first_y + n: n for n in range(n_sums)} if has_y and not narrow else {},
        compiler_params=pltpu.CompilerParams(vmem_limit_bytes=VMEM_BYTES),
        cost_estimate=pl.CostEstimate(flops=rows * total * feat, bytes_accessed=width * total, transcendentals=0),
    )(*operands)


def finish_kernel(feat, home_ref, low_ref, high_ref, *out_refs):
    def write(back_ref):
        for f, out in enumerate(out_refs):
            b = slice(f * feat, (f + 1) * feat)
            out[...] = NMAT * (home_ref[:, b] + back_ref[:, b].astype(jnp.float32))

    steps = pl.num_programs(0) // 2
    pl.when(pl.program_id(0) < steps)(lambda: write(low_ref))
    pl.when(pl.program_id(0) >= steps)(lambda: write(high_ref))


def finish(home, low, high):
    rows, width = home.shape
    feat = width // 3
    steps = low.shape[0] // LANES
    return pl.pallas_call(
        functools.partial(finish_kernel, feat),
        grid=(2 * steps,),
        in_specs=[
            pl.BlockSpec((LANES, width), lambda i: (i, 0)),
            pl.BlockSpec((LANES, width), lambda i: (jnp.minimum(i, steps - 1), 0)),
            pl.BlockSpec((LANES, width), lambda i: (jnp.maximum(i - steps, 0), 0)),
        ],
        out_specs=[pl.BlockSpec((LANES, feat), lambda i: (i, 0))] * 3,
        out_shape=[jax.ShapeDtypeStruct((rows, feat), jnp.float32)] * 3,
        compiler_params=pltpu.CompilerParams(vmem_limit_bytes=VMEM_BYTES),
        cost_estimate=pl.CostEstimate(flops=rows * width, bytes_accessed=rows * width * 10, transcendentals=0),
    )(home, low, high)


def near_shards(factor_a, factor_b, factor_c):
    x = jnp.concatenate([factor_a, factor_b, factor_c], axis=1)
    rows = x.shape[0]
    early = rows * 5 // 8
    row = lax.axis_index("row")
    inner = (row >= 2) & (row < 6)
    fence = lax.optimization_barrier

    def move(axis, pairs):
        return lambda v: lax.ppermute(v, axis, pairs)

    core = move("row", [(r, r ^ 1) for r in range(8)])
    partner = move("row", [(r, r ^ 2) for r in range(8)])
    across = move("row", [(2, 4), (3, 5), (4, 2), (5, 3)])
    outward = move("row", [(2, 0), (3, 1), (4, 6), (5, 7)])
    along_x = move("col", [(c, c ^ 1) for c in range(4)])
    along_y = move("col", [(c, c ^ 2) for c in range(4)])

    def corner(from_x, from_y):
        mid = from_x.shape[0] // 2
        return along_x(from_y[:mid]), along_y(from_x[mid:])

    x_x, x_y, x_s = along_x(x), along_y(x), core(x)
    part_a, part_c = x[:early], x[early:]
    guest_a, far_a = partner(part_a), across(part_a)
    home = trace_terms(x)
    (home,) = pair_sums([x], [x, x_s], [home], 1024)
    guest_a, far_a, part_c, home = fence((guest_a, far_a, part_c, home))

    guest_c, far_c = partner(part_c), across(part_c)
    x_x, x_y, guest_c, far_c = fence((x_x, x_y, guest_c, far_c))

    guest = [guest_a, guest_c]
    x_d0, x_d1 = corner(x_x, x_y)
    out_a, next_b = outward(far_a), across(guest_a)
    x_xs, x_ys = core(x_x), core(x_y)
    (visit,) = pair_sums(guest, [x, x_s, x_x, x_y, x_xs, x_ys], None, 1024)
    x_d0, x_d1, out_a, next_b, visit = fence((x_d0, x_d1, out_a, next_b, visit))

    e = jnp.where(inner, next_b, out_a)
    e_x, e_y = along_x(e), along_y(e)
    out_c0, next_c = outward(far_c), across(guest_c)
    x_ds0, x_ds1, e_s = fence((core(x_d0), core(x_d1), core(e)))
    x_d = [x_d0, x_d1, x_ds0, x_ds1]
    (home,) = pair_sums([x], [x_x, x_y, x_xs, x_ys, *x_d], [home], 1024)
    e_x, e_y, next_c, home = fence((e_x, e_y, next_c, home))

    e_d0, e_d1 = corner(e_x, e_y)
    out_c1 = outward(next_c)
    e_xs, e_ys = fence((core(e_x), core(e_y)))
    lead = 3 * rows - 4 * early
    (visit,) = pair_sums(guest, [*x_d, e, e_s, e_x, e_y, (e_xs, 0, lead)], [visit], 1280)
    e_d0, e_d1, out_c0, out_c1, visit = fence((e_d0, e_d1, out_c0, out_c1, visit))

    c = jnp.where(inner, jnp.concatenate([far_c, next_c]), jnp.concatenate([out_c0, out_c1]))
    c_x, c_y = along_x(c), along_y(c)
    e_ds0, e_ds1, c_s = fence((core(e_d0), core(e_d1), core(c)))
    e_d = [e_d0, e_d1, e_ds0, e_ds1]
    visit_0, visit_1 = pair_sums(guest, [(e_xs, lead, early - lead), e_ys, *e_d], [visit], 1024, narrow=True)
    visit_0, visit_1, home = fence((visit_0, visit_1, home))
    back_0 = partner(visit_0)
    (home,) = pair_sums([x], [e, e_s, e_x, e_y, e_xs, e_ys, *e_d], [home], 1280)
    c_x, c_y, back_0, visit_1, home = fence((c_x, c_y, back_0, visit_1, home))

    back_1 = partner(visit_1)
    c_d0, c_d1 = corner(c_x, c_y)
    (home,) = pair_sums([x], [c, c_s, c_x, c_y, core(c_x), core(c_y)], [home], 768)
    c_d0, c_d1, home = fence((c_d0, c_d1, home))
    (home,) = pair_sums([x], [c_d0, c_d1, core(c_d0), core(c_d1)], [home], 768)
    return tuple(finish(home, back_0, back_1))


def gram_rows(left, right):
    return lax.dot_general(
        left, right, (((1,), (1,)), ((), ())), preferred_element_type=jnp.float32
    )


def apply_rows(hadam, right):
    return jnp.dot(hadam, right, preferred_element_type=jnp.float32)


def block_terms(lefts, rights):
    grams = [gram_rows(l, r) for l, r in zip(lefts, rights)]
    hadam_a = (grams[1] * grams[2]).astype(jnp.bfloat16)
    hadam_b = (grams[2] * grams[0]).astype(jnp.bfloat16)
    hadam_c = (grams[0] * grams[1]).astype(jnp.bfloat16)
    hadams = (hadam_a, hadam_b, hadam_c)
    return jnp.concatenate([apply_rows(h, r) for h, r in zip(hadams, rights)], axis=1)


def shards(factor_a, factor_b, factor_c):
    own_rows = factor_a.shape[0]
    length = factor_a.shape[1]
    block_j = (
        lax.all_gather(factor_a, "row", axis=0, tiled=True),
        lax.all_gather(factor_b, "row", axis=0, tiled=True),
        lax.all_gather(factor_c, "row", axis=0, tiled=True),
    )
    block_i = (
        lax.all_gather(factor_a, "col", axis=0, tiled=True),
        lax.all_gather(factor_b, "col", axis=0, tiled=True),
        lax.all_gather(factor_c, "col", axis=0, tiled=True),
    )
    lefts = [x for x in block_i]
    summed = lax.psum_scatter(
        block_terms(lefts, block_j).astype(jnp.bfloat16), "col", scatter_dimension=0, tiled=True
    ).astype(jnp.float32)
    cube_a = factor_a.astype(jnp.float32).reshape(own_rows, NMAT, NMAT)
    cube_b = factor_b.astype(jnp.float32).reshape(own_rows, NMAT, NMAT)
    cube_c = factor_c.astype(jnp.float32).reshape(own_rows, NMAT, NMAT)
    data_a = jnp.einsum("rjk,rki->rij", cube_b, cube_c).reshape(own_rows, length)
    data_b = jnp.einsum("rki,rij->rjk", cube_c, cube_a).reshape(own_rows, length)
    data_c = jnp.einsum("rij,rjk->rki", cube_a, cube_b).reshape(own_rows, length)
    grad_a = NMAT * (summed[:, :length] - data_a)
    grad_b = NMAT * (summed[:, length : 2 * length] - data_b)
    grad_c = NMAT * (summed[:, 2 * length :] - data_c)
    return (grad_a, grad_b, grad_c)


def solution(mesh):
    spec = P(("col", "row"), None)
    near = (mesh.shape["row"], mesh.shape["col"]) == (8, 4)
    return jax.shard_map(
        near_shards if near else shards, mesh=mesh, in_specs=(spec,) * 3, out_specs=(spec,) * 3, check_vma=False
    )
```

```python
import functools

import jax
import jax.numpy as jnp
from jax import lax
from jax.experimental import pallas as pl
from jax.experimental.pallas import tpu as pltpu
from jax.sharding import PartitionSpec as P

NMAT = 32
ROW_TILE = 256
LANES = 128
VMEM_BYTES = 60 * 1024 * 1024


def trace_kernel(feat, x_ref, out_ref, left, right, prod):
    blocks = [slice(f * feat, (f + 1) * feat) for f in range(3)]
    for out, (l, r) in enumerate(((1, 2), (2, 0), (0, 1))):
        left[...] = x_ref[:, blocks[l]].astype(jnp.float32).T
        right[...] = x_ref[:, blocks[r]].astype(jnp.float32).T

        def rows(step, carry):
            base = step * 4
            sums = [None] * 4
            for k in range(NMAT):
                line = right[k * NMAT : (k + 1) * NMAT, :]
                for n in range(4):
                    term = left[pl.ds((base + n) * NMAT + k, 1), :] * line
                    sums[n] = term if k == 0 else sums[n] + term
            for n in range(4):
                prod[pl.ds(base + n, NMAT, stride=NMAT), :] = sums[n]
            return carry

        lax.fori_loop(0, NMAT // 4, rows, 0)
        out_ref[:, blocks[out]] = -prod[...].T


def trace_terms(x):
    rows, width = x.shape
    feat = width // 3
    spec = pl.BlockSpec((LANES, width), lambda i: (i, 0))
    return pl.pallas_call(
        functools.partial(trace_kernel, feat),
        grid=(rows // LANES,),
        in_specs=[spec],
        out_specs=spec,
        out_shape=jax.ShapeDtypeStruct((rows, width), jnp.float32),
        scratch_shapes=[pltpu.VMEM((feat, LANES), jnp.float32)] * 3,
        compiler_params=pltpu.CompilerParams(vmem_limit_bytes=VMEM_BYTES),
        cost_estimate=pl.CostEstimate(flops=rows, bytes_accessed=width, transcendentals=0),
    )(x)


def pair_kernel(feat, i_rows, spans, tile, n_sums, narrow, has_y, final, *refs):
    refs = list(refs)
    take = lambda n: [refs.pop(0) for _ in range(n)]
    tiles = sum(count for _, count in spans) // tile
    n_i = sum(i_rows) // ROW_TILE
    per = n_i // n_sums
    blocks = [slice(f * feat, (f + 1) * feat) for f in range(3)]
    i_refs, j_refs = take(len(i_rows)), take(len(spans))
    y_refs = take(n_sums) if has_y else []
    back_refs = take(n_i) if final else []
    out_refs = take(n_i if narrow else 3 if final else n_sums)
    ibuf, jbuf, acc, i_sem, j_sem, y_sem, o_sem = take(7)
    packed, b_sem = take(2) if narrow or final else (None, None)

    def block(i):
        return pl.ds(i * ROW_TILE, ROW_TILE)

    def fill(buf, sem, sources, ranges, t, size):
        low = 0
        for ref, (first, count) in zip(sources, ranges):
            a, b = max(low, t * size), min(low + count, (t + 1) * size)
            if a < b:
                src = ref.at[pl.ds(first + a - low, b - a)]
                pltpu.make_async_copy(src, buf.at[pl.ds(a, b - a)], sem.at[t]).start()
            low += count

    fill(jbuf, j_sem, j_refs, spans, 0, tile)
    for i in range(n_i):
        fill(ibuf, i_sem, i_refs, [(0, count) for count in i_rows], i, ROW_TILE)
        if has_y:
            pltpu.make_async_copy(y_refs[i // per].at[block(i % per)], acc.at[block(i)], y_sem.at[i]).start()
    for t in range(1, tiles):
        fill(jbuf, j_sem, j_refs, spans, t, tile)
    for i, ref in enumerate(back_refs):
        pltpu.make_async_copy(ref, packed.at[block(i)], b_sem.at[i]).start()

    def wait(ref, sem):
        pltpu.make_async_copy(ref, ref, sem).wait()

    def over_tiles(t, carry):
        cols = pl.ds(pl.multiple_of(t * tile, tile), tile)
        wait(jbuf.at[cols], j_sem.at[t])

        def over_rows(i, inner):
            span = pl.ds(pl.multiple_of(i * ROW_TILE, ROW_TILE), ROW_TILE)

            @pl.when(t == 0)
            def _():
                wait(ibuf.at[span], i_sem.at[i])

            grams = [
                lax.dot_general(ibuf[span, b], jbuf[cols, b], (((1,), (1,)), ((), ())), preferred_element_type=jnp.float32)
                for b in blocks
            ]
            hadams = [(grams[(f + 1) % 3] * grams[(f + 2) % 3]).astype(jnp.bfloat16) for f in range(3)]

            @pl.when(t == 0)
            def _():
                if has_y:
                    wait(acc.at[span], y_sem.at[i])
                else:
                    acc[span, :] = jnp.zeros((ROW_TILE, 3 * feat), jnp.float32)

            for hadam, b in zip(hadams, blocks):
                acc[span, b] += jnp.dot(hadam, jbuf[cols, b], preferred_element_type=jnp.float32)

            @pl.when(t == tiles - 1)
            def _():
                if final:
                    wait(packed.at[span], b_sem.at[i])
                    acc[span, :] = NMAT * (acc[span, :] + packed[span, :].astype(jnp.float32))
                    for out, b in zip(out_refs, blocks):
                        pltpu.make_async_copy(acc.at[span, b], out.at[span], o_sem.at[i]).start()
                for n in range(0 if final else n_i):
                    @pl.when(i == n)
                    def _():
                        if narrow:
                            packed[block(n), :] = acc[block(n), :].astype(jnp.bfloat16)
                            src, dst = packed.at[block(n)], out_refs[n]
                        else:
                            src, dst = acc.at[block(n)], out_refs[n // per].at[block(n % per)]
                        pltpu.make_async_copy(src, dst, o_sem.at[n]).start()
            return inner

        return lax.fori_loop(0, n_i, over_rows, carry)

    lax.fori_loop(0, tiles, over_tiles, 0)
    for i in range(n_i):
        wait((packed if narrow else acc).at[block(i)], o_sem.at[i])


def pair_sums(lefts, rights, sums, tile, narrow=False, back=None):
    width = lefts[0].shape[1]
    feat = width // 3
    i_rows = [v.shape[0] for v in lefts]
    rows = sum(i_rows)
    rights = [r if isinstance(r, tuple) else (r, 0, r.shape[0]) for r in rights]
    spans = [(first, count) for _, first, count in rights]
    total = sum(count for _, count in spans)
    assert total % tile == 0 and rows % ROW_TILE == 0
    n_i = rows // ROW_TILE
    has_y, final = sums is not None, back is not None
    n_sums = len(sums) if has_y else 1
    any_spec = pl.BlockSpec(memory_space=pltpu.HBM)
    operands = [*lefts, *(r for r, _, _ in rights), *(sums or []), *(back or [])]
    first_y = len(lefts) + len(rights)
    if narrow:
        outs = [jax.ShapeDtypeStruct((ROW_TILE, width), jnp.bfloat16)] * n_i
    elif final:
        outs = [jax.ShapeDtypeStruct((rows, feat), jnp.float32)] * 3
    else:
        outs = [jax.ShapeDtypeStruct((rows // n_sums, width), jnp.float32)] * n_sums
    scratch = [
        pltpu.VMEM((rows, width), jnp.bfloat16),
        pltpu.VMEM((total, width), jnp.bfloat16),
        pltpu.VMEM((rows, width), jnp.float32),
        pltpu.SemaphoreType.DMA((n_i,)),
        pltpu.SemaphoreType.DMA((total // tile,)),
        pltpu.SemaphoreType.DMA((n_i,)),
        pltpu.SemaphoreType.DMA((n_i,)),
    ]
    if narrow or final:
        scratch += [pltpu.VMEM((rows, width), jnp.bfloat16), pltpu.SemaphoreType.DMA((n_i,))]
    return pl.pallas_call(
        functools.partial(pair_kernel, feat, i_rows, spans, tile, n_sums, narrow, has_y, final),
        in_specs=[any_spec] * len(operands),
        out_specs=[any_spec] * len(outs),
        out_shape=outs,
        scratch_shapes=scratch,
        input_output_aliases={first_y + n: n for n in range(n_sums)} if has_y and not narrow and not final else {},
        compiler_params=pltpu.CompilerParams(vmem_limit_bytes=VMEM_BYTES),
        cost_estimate=pl.CostEstimate(flops=rows, bytes_accessed=width, transcendentals=0),
    )(*operands)


def cut_kernel(mid, parts, x_ref, y_ref, low_ref, high_ref, low, high, sem):
    size = mid // parts
    spans = [pl.ds(n * size, size) for n in range(parts)]
    moves = []
    for n, span in enumerate(spans):
        moves.append((y_ref.at[span], low.at[span], low_ref.at[span], n))
        moves.append((x_ref.at[pl.ds(mid + n * size, size)], high.at[span], high_ref.at[span], parts + n))
    first = [pltpu.make_async_copy(src, buf, sem.at[0, n]) for src, buf, _, n in moves]
    last = [pltpu.make_async_copy(buf, dst, sem.at[1, n]) for _, buf, dst, n in moves]
    for copy in first:
        copy.start()
    for copy, then in zip(first, last):
        copy.wait()
        then.start()
    for copy in last:
        copy.wait()


def cut(from_x, from_y):
    rows, width = from_x.shape
    mid, parts = rows // 2, 2
    spec = pl.BlockSpec(memory_space=pltpu.HBM)
    return pl.pallas_call(
        functools.partial(cut_kernel, mid, parts),
        in_specs=[spec] * 2,
        out_specs=[spec] * 2,
        out_shape=[jax.ShapeDtypeStruct((mid, width), from_x.dtype)] * 2,
        scratch_shapes=[pltpu.VMEM((mid, width), from_x.dtype)] * 2 + [pltpu.SemaphoreType.DMA((2, 2 * parts))],
        cost_estimate=pl.CostEstimate(flops=0, bytes_accessed=rows * width, transcendentals=0),
    )(from_x, from_y)


def near_shards(factor_a, factor_b, factor_c):
    x = jnp.concatenate([factor_a, factor_b, factor_c], axis=1)
    rows = x.shape[0]
    early = rows * 5 // 8
    row = lax.axis_index("row")
    inner = (row >= 2) & (row < 6)
    fence = lax.optimization_barrier

    def move(axis, pairs):
        return lambda v: lax.ppermute(v, axis, pairs)

    core = move("row", [(r, r ^ 1) for r in range(8)])
    partner = move("row", [(r, r ^ 2) for r in range(8)])
    across = move("row", [(2, 4), (3, 5), (4, 2), (5, 3)])
    outward = move("row", [(2, 0), (3, 1), (4, 6), (5, 7)])
    along_x = move("col", [(c, c ^ 1) for c in range(4)])
    along_y = move("col", [(c, c ^ 2) for c in range(4)])

    def corner(from_x, from_y):
        low, high = cut(from_x, from_y)
        return along_x(low), along_y(high)

    x_x, x_y, x_s = along_x(x), along_y(x), core(x)
    x_z, x_s = fence((x, x_s))
    part_a, part_c = x_z[:early], x_z[early:]
    guest_a, far_a = partner(part_a), across(part_a)
    home = trace_terms(x)
    (home,) = pair_sums([x], [x, x_s], [home], 1024)
    guest_a, far_a, home = fence((guest_a, far_a, home))

    out_a, next_b = outward(far_a), across(guest_a)
    x_x, x_y, home = fence((x_x, x_y, home))

    x_d0, x_d1 = corner(x_x, x_y)
    x_xs, x_ys = fence((core(x_x), core(x_y)))
    (home,) = pair_sums([x], [x_x, x_y, x_xs, x_ys], [home], 1024)
    out_a, next_b, part_c, home = fence((out_a, next_b, part_c, home))

    guest_c, far_c = partner(part_c), across(part_c)
    x_d0, x_d1, out_a, next_b, home = fence((x_d0, x_d1, out_a, next_b, home))

    e = jnp.where(inner, next_b, out_a)
    e_x, e_y = along_x(e), along_y(e)
    x_ds0, x_ds1, e_s = fence((core(x_d0), core(x_d1), core(e)))
    x_d = [x_d0, x_d1, x_ds0, x_ds1]
    (home,) = pair_sums([x], x_d, [home], 1024)
    guest_c, far_c, home = fence((guest_c, far_c, home))

    guest = [guest_a, guest_c]
    out_c0, next_c = outward(far_c), across(guest_c)
    (visit,) = pair_sums(guest, [x, x_s, x_x, x_y, x_xs, x_ys], None, 1024)
    e_x, e_y, out_c0, next_c, home, visit = fence((e_x, e_y, out_c0, next_c, home, visit))

    e_d0, e_d1 = corner(e_x, e_y)
    out_c1 = outward(next_c)
    e_xs, e_ys = fence((core(e_x), core(e_y)))
    lead = 3 * rows - 4 * early
    (visit,) = pair_sums(guest, [*x_d, e, e_s, e_x, e_y, (e_xs, 0, lead)], [visit], 1280)
    e_d0, e_d1, out_c1, visit = fence((e_d0, e_d1, out_c1, visit))

    c = jnp.where(inner, jnp.concatenate([far_c, next_c]), jnp.concatenate([out_c0, out_c1]))
    c_x, c_y = along_x(c), along_y(c)
    e_ds0, e_ds1, c_s = fence((core(e_d0), core(e_d1), core(c)))
    e_d = [e_d0, e_d1, e_ds0, e_ds1]
    visit_0, visit_1 = pair_sums(guest, [(e_xs, lead, early - lead), e_ys, *e_d], [visit], 1024, narrow=True)
    visit_0, visit_1, home = fence((visit_0, visit_1, home))
    back_0 = partner(visit_0)
    (home,) = pair_sums([x], [e, e_s, e_x, e_y, e_xs, e_ys, *e_d], [home], 1280)
    c_x, c_y, back_0, visit_1, home = fence((c_x, c_y, back_0, visit_1, home))

    back_1 = partner(visit_1)
    c_d0, c_d1 = corner(c_x, c_y)
    (home,) = pair_sums([x], [c, c_s, c_x, c_y, core(c_x), core(c_y)], [home], 768)
    c_d0, c_d1, home = fence((c_d0, c_d1, home))
    c_d = [c_d0, c_d1, core(c_d0), core(c_d1)]
    return tuple(pair_sums([x], c_d, [home], 768, back=[back_0, back_1]))


def gram_rows(left, right):
    return lax.dot_general(
        left, right, (((1,), (1,)), ((), ())), preferred_element_type=jnp.float32
    )


def apply_rows(hadam, right):
    return jnp.dot(hadam, right, preferred_element_type=jnp.float32)


def block_terms(lefts, rights):
    grams = [gram_rows(l, r) for l, r in zip(lefts, rights)]
    hadam_a = (grams[1] * grams[2]).astype(jnp.bfloat16)
    hadam_b = (grams[2] * grams[0]).astype(jnp.bfloat16)
    hadam_c = (grams[0] * grams[1]).astype(jnp.bfloat16)
    hadams = (hadam_a, hadam_b, hadam_c)
    return jnp.concatenate([apply_rows(h, r) for h, r in zip(hadams, rights)], axis=1)


def shards(factor_a, factor_b, factor_c):
    own_rows = factor_a.shape[0]
    length = factor_a.shape[1]
    block_j = (
        lax.all_gather(factor_a, "row", axis=0, tiled=True),
        lax.all_gather(factor_b, "row", axis=0, tiled=True),
        lax.all_gather(factor_c, "row", axis=0, tiled=True),
    )
    block_i = (
        lax.all_gather(factor_a, "col", axis=0, tiled=True),
        lax.all_gather(factor_b, "col", axis=0, tiled=True),
        lax.all_gather(factor_c, "col", axis=0, tiled=True),
    )
    lefts = [x for x in block_i]
    summed = lax.psum_scatter(
        block_terms(lefts, block_j).astype(jnp.bfloat16), "col", scatter_dimension=0, tiled=True
    ).astype(jnp.float32)
    cube_a = factor_a.astype(jnp.float32).reshape(own_rows, NMAT, NMAT)
    cube_b = factor_b.astype(jnp.float32).reshape(own_rows, NMAT, NMAT)
    cube_c = factor_c.astype(jnp.float32).reshape(own_rows, NMAT, NMAT)
    data_a = jnp.einsum("rjk,rki->rij", cube_b, cube_c).reshape(own_rows, length)
    data_b = jnp.einsum("rki,rij->rjk", cube_c, cube_a).reshape(own_rows, length)
    data_c = jnp.einsum("rij,rjk->rki", cube_a, cube_b).reshape(own_rows, length)
    grad_a = NMAT * (summed[:, :length] - data_a)
    grad_b = NMAT * (summed[:, length : 2 * length] - data_b)
    grad_c = NMAT * (summed[:, 2 * length :] - data_c)
    return (grad_a, grad_b, grad_c)


def solution(mesh):
    spec = P(("col", "row"), None)
    near = (mesh.shape["row"], mesh.shape["col"]) == (8, 4)
    return jax.shard_map(
        near_shards if near else shards, mesh=mesh, in_specs=(spec,) * 3, out_specs=(spec,) * 3, check_vma=False
    )
```

```python
import functools

import jax
import jax.numpy as jnp
from jax import lax
from jax.experimental import pallas as pl
from jax.experimental.pallas import tpu as pltpu
from jax.sharding import PartitionSpec as P

NMAT = 32
ROW_TILE = 256
LANES = 128
VMEM_BYTES = 63 * 1024 * 1024 + 512 * 1024


def trace_kernel(feat, x_ref, out_ref, left, right, prod):
    blocks = [slice(f * feat, (f + 1) * feat) for f in range(3)]
    for out, (l, r) in enumerate(((1, 2), (2, 0), (0, 1))):
        left[...] = x_ref[:, blocks[l]].astype(jnp.float32).T
        right[...] = x_ref[:, blocks[r]].astype(jnp.float32).T

        def rows(step, carry):
            base = step * 4
            sums = [None] * 4
            for k in range(NMAT):
                line = right[k * NMAT : (k + 1) * NMAT, :]
                for n in range(4):
                    term = left[pl.ds((base + n) * NMAT + k, 1), :] * line
                    sums[n] = term if k == 0 else sums[n] + term
            for n in range(4):
                prod[pl.ds(base + n, NMAT, stride=NMAT), :] = sums[n]
            return carry

        lax.fori_loop(0, NMAT // 4, rows, 0)
        out_ref[:, blocks[out]] = -prod[...].T


def trace_terms(x):
    rows, width = x.shape
    feat = width // 3
    spec = pl.BlockSpec((LANES, width), lambda i: (i, 0))
    return pl.pallas_call(
        functools.partial(trace_kernel, feat),
        grid=(rows // LANES,),
        in_specs=[spec],
        out_specs=spec,
        out_shape=jax.ShapeDtypeStruct((rows, width), jnp.float32),
        scratch_shapes=[pltpu.VMEM((feat, LANES), jnp.float32)] * 3,
        compiler_params=pltpu.CompilerParams(vmem_limit_bytes=VMEM_BYTES),
        cost_estimate=pl.CostEstimate(flops=rows, bytes_accessed=width, transcendentals=0),
    )(x)


def pair_kernel(feat, i_rows, spans, tile, n_sums, narrow, has_y, final, *refs):
    refs = list(refs)
    take = lambda n: [refs.pop(0) for _ in range(n)]
    tiles = sum(count for _, count in spans) // tile
    n_i = sum(i_rows) // ROW_TILE
    per = n_i // n_sums
    blocks = [slice(f * feat, (f + 1) * feat) for f in range(3)]
    i_refs, j_refs = take(len(i_rows)), take(len(spans))
    y_refs = take(n_sums) if has_y else []
    back_refs = take(n_i) if final else []
    out_refs = take(n_i if narrow else 3 if final else n_sums)
    ibuf, jbuf, acc, i_sem, j_sem, y_sem, o_sem = take(7)
    packed, b_sem = take(2) if narrow or final else (None, None)

    def block(i):
        return pl.ds(i * ROW_TILE, ROW_TILE)

    def fill(buf, sem, sources, ranges, t, size):
        low = 0
        for ref, (first, count) in zip(sources, ranges):
            a, b = max(low, t * size), min(low + count, (t + 1) * size)
            if a < b:
                src = ref.at[pl.ds(first + a - low, b - a)]
                pltpu.make_async_copy(src, buf.at[pl.ds(a, b - a)], sem.at[t]).start()
            low += count

    fill(jbuf, j_sem, j_refs, spans, 0, tile)
    for i in range(n_i):
        fill(ibuf, i_sem, i_refs, [(0, count) for count in i_rows], i, ROW_TILE)
        if has_y:
            pltpu.make_async_copy(y_refs[i // per].at[block(i % per)], acc.at[block(i)], y_sem.at[i]).start()
    for t in range(1, tiles):
        fill(jbuf, j_sem, j_refs, spans, t, tile)
    for i, ref in enumerate(back_refs):
        pltpu.make_async_copy(ref, packed.at[block(i)], b_sem.at[i]).start()

    def wait(ref, sem):
        pltpu.make_async_copy(ref, ref, sem).wait()

    def over_tiles(t, carry):
        cols = pl.ds(pl.multiple_of(t * tile, tile), tile)
        wait(jbuf.at[cols], j_sem.at[t])

        def over_rows(i, inner):
            span = pl.ds(pl.multiple_of(i * ROW_TILE, ROW_TILE), ROW_TILE)

            @pl.when(t == 0)
            def _():
                wait(ibuf.at[span], i_sem.at[i])

            grams = [
                lax.dot_general(ibuf[span, b], jbuf[cols, b], (((1,), (1,)), ((), ())), preferred_element_type=jnp.float32)
                for b in blocks
            ]
            hadams = [(grams[(f + 1) % 3] * grams[(f + 2) % 3]).astype(jnp.bfloat16) for f in range(3)]

            @pl.when(t == 0)
            def _():
                if has_y:
                    wait(acc.at[span], y_sem.at[i])
                else:
                    acc[span, :] = jnp.zeros((ROW_TILE, 3 * feat), jnp.float32)

            for hadam, b in zip(hadams, blocks):
                acc[span, b] += jnp.dot(hadam, jbuf[cols, b], preferred_element_type=jnp.float32)

            @pl.when(t == tiles - 1)
            def _():
                if final:
                    wait(packed.at[span], b_sem.at[i])
                    acc[span, :] = NMAT * (acc[span, :] + packed[span, :].astype(jnp.float32))
                    for out, b in zip(out_refs, blocks):
                        pltpu.make_async_copy(acc.at[span, b], out.at[span], o_sem.at[i]).start()
                for n in range(0 if final else n_i):
                    @pl.when(i == n)
                    def _():
                        if narrow:
                            packed[block(n), :] = acc[block(n), :].astype(jnp.bfloat16)
                            src, dst = packed.at[block(n)], out_refs[n]
                        else:
                            src, dst = acc.at[block(n)], out_refs[n // per].at[block(n % per)]
                        pltpu.make_async_copy(src, dst, o_sem.at[n]).start()
            return inner

        return lax.fori_loop(0, n_i, over_rows, carry)

    lax.fori_loop(0, tiles, over_tiles, 0)
    for i in range(n_i):
        wait((packed if narrow else acc).at[block(i)], o_sem.at[i])


def pair_sums(lefts, rights, sums, tile, narrow=False, back=None):
    width = lefts[0].shape[1]
    feat = width // 3
    i_rows = [v.shape[0] for v in lefts]
    rows = sum(i_rows)
    rights = [r if isinstance(r, tuple) else (r, 0, r.shape[0]) for r in rights]
    spans = [(first, count) for _, first, count in rights]
    total = sum(count for _, count in spans)
    assert total % tile == 0 and rows % ROW_TILE == 0
    n_i = rows // ROW_TILE
    has_y, final = sums is not None, back is not None
    n_sums = len(sums) if has_y else 1
    any_spec = pl.BlockSpec(memory_space=pltpu.HBM)
    operands = [*lefts, *(r for r, _, _ in rights), *(sums or []), *(back or [])]
    first_y = len(lefts) + len(rights)
    if narrow:
        outs = [jax.ShapeDtypeStruct((ROW_TILE, width), jnp.bfloat16)] * n_i
    elif final:
        outs = [jax.ShapeDtypeStruct((rows, feat), jnp.float32)] * 3
    else:
        outs = [jax.ShapeDtypeStruct((rows // n_sums, width), jnp.float32)] * n_sums
    scratch = [
        pltpu.VMEM((rows, width), jnp.bfloat16),
        pltpu.VMEM((total, width), jnp.bfloat16),
        pltpu.VMEM((rows, width), jnp.float32),
        pltpu.SemaphoreType.DMA((n_i,)),
        pltpu.SemaphoreType.DMA((total // tile,)),
        pltpu.SemaphoreType.DMA((n_i,)),
        pltpu.SemaphoreType.DMA((n_i,)),
    ]
    if narrow or final:
        scratch += [pltpu.VMEM((rows, width), jnp.bfloat16), pltpu.SemaphoreType.DMA((n_i,))]
    return pl.pallas_call(
        functools.partial(pair_kernel, feat, i_rows, spans, tile, n_sums, narrow, has_y, final),
        in_specs=[any_spec] * len(operands),
        out_specs=[any_spec] * len(outs),
        out_shape=outs,
        scratch_shapes=scratch,
        input_output_aliases={first_y + n: n for n in range(n_sums)} if has_y and not narrow and not final else {},
        compiler_params=pltpu.CompilerParams(vmem_limit_bytes=VMEM_BYTES),
        cost_estimate=pl.CostEstimate(flops=rows, bytes_accessed=width, transcendentals=0),
    )(*operands)


def cut_kernel(mid, parts, x_ref, y_ref, low_ref, high_ref, low, high, sem):
    size = mid // parts
    spans = [pl.ds(n * size, size) for n in range(parts)]
    moves = []
    for n, span in enumerate(spans):
        moves.append((y_ref.at[span], low.at[span], low_ref.at[span], n))
        moves.append((x_ref.at[pl.ds(mid + n * size, size)], high.at[span], high_ref.at[span], parts + n))
    first = [pltpu.make_async_copy(src, buf, sem.at[0, n]) for src, buf, _, n in moves]
    last = [pltpu.make_async_copy(buf, dst, sem.at[1, n]) for _, buf, dst, n in moves]
    for copy in first:
        copy.start()
    for copy, then in zip(first, last):
        copy.wait()
        then.start()
    for copy in last:
        copy.wait()


def cut(from_x, from_y):
    rows, width = from_x.shape
    mid, parts = rows // 2, 2
    spec = pl.BlockSpec(memory_space=pltpu.HBM)
    return pl.pallas_call(
        functools.partial(cut_kernel, mid, parts),
        in_specs=[spec] * 2,
        out_specs=[spec] * 2,
        out_shape=[jax.ShapeDtypeStruct((mid, width), from_x.dtype)] * 2,
        scratch_shapes=[pltpu.VMEM((mid, width), from_x.dtype)] * 2 + [pltpu.SemaphoreType.DMA((2, 2 * parts))],
        cost_estimate=pl.CostEstimate(flops=0, bytes_accessed=rows * width, transcendentals=0),
    )(from_x, from_y)


def join_kernel(parts, a_ref, b_ref, c_ref, out_ref, low_ref, high_ref, buf, sem):
    rows, feat = a_ref.shape
    size = rows // parts
    spans = [pl.ds(n * size, size) for n in range(parts)]
    loads = [
        [
            pltpu.make_async_copy(ref.at[span], buf.at[span, pl.ds(f * feat, feat)], sem.at[f, n])
            for f, ref in enumerate((a_ref, b_ref, c_ref))
        ]
        for n, span in enumerate(spans)
    ]
    stores = [pltpu.make_async_copy(buf.at[span], out_ref.at[span], sem.at[3, n]) for n, span in enumerate(spans)]
    for copies in loads:
        for copy in copies:
            copy.start()
    for copies, store in zip(loads, stores):
        for copy in copies:
            copy.wait()
        store.start()
    low = low_ref.shape[0]
    stores.append(pltpu.make_async_copy(buf.at[pl.ds(0, low)], low_ref, sem.at[4, 0]))
    stores.append(pltpu.make_async_copy(buf.at[pl.ds(low, rows - low)], high_ref, sem.at[4, 1]))
    for store in stores[-2:]:
        store.start()
    for store in stores:
        store.wait()


def side_by_side(a, b, c, low):
    rows, feat = a.shape
    parts = 4
    spec = pl.BlockSpec(memory_space=pltpu.HBM)
    outs = [jax.ShapeDtypeStruct((n, 3 * feat), a.dtype) for n in (rows, low, rows - low)]
    return pl.pallas_call(
        functools.partial(join_kernel, parts),
        in_specs=[spec] * 3,
        out_specs=[spec] * 3,
        out_shape=outs,
        scratch_shapes=[pltpu.VMEM(outs[0].shape, a.dtype), pltpu.SemaphoreType.DMA((5, parts))],
        cost_estimate=pl.CostEstimate(flops=rows, bytes_accessed=feat, transcendentals=0),
    )(a, b, c)


def near_shards(factor_a, factor_b, factor_c):
    rows = factor_a.shape[0]
    early = rows * 5 // 8
    x, part_a, part_c = side_by_side(factor_a, factor_b, factor_c, early)
    row = lax.axis_index("row")
    inner = (row >= 2) & (row < 6)
    fence = lax.optimization_barrier

    def move(axis, pairs):
        return lambda v: lax.ppermute(v, axis, pairs)

    core = move("row", [(r, r ^ 1) for r in range(8)])
    partner = move("row", [(r, r ^ 2) for r in range(8)])
    across = move("row", [(2, 4), (3, 5), (4, 2), (5, 3)])
    outward = move("row", [(2, 0), (3, 1), (4, 6), (5, 7)])
    along_x = move("col", [(c, c ^ 1) for c in range(4)])
    along_y = move("col", [(c, c ^ 2) for c in range(4)])

    def corner(from_x, from_y):
        low, high = cut(from_x, from_y)
        return along_x(low), along_y(high)

    x_x, x_y, x_s = along_x(x), along_y(x), core(x)
    guest_a, far_a = partner(part_a), across(part_a)
    home = trace_terms(x)
    (home,) = pair_sums([x], [x, x_s], [home], 1024)
    guest_a, far_a, part_c, home = fence((guest_a, far_a, part_c, home))

    guest_c, far_c = partner(part_c), across(part_c)
    x_x, x_y, guest_c, far_c, home = fence((x_x, x_y, guest_c, far_c, home))

    guest = [guest_a, guest_c]
    out_a, next_b = outward(far_a), across(guest_a)
    x_d0, x_d1 = corner(x_x, x_y)
    x_xs, x_ys = fence((core(x_x), core(x_y)))
    (visit,) = pair_sums(guest, [x, x_s, x_x, x_y, x_xs, x_ys], None, 1024)
    x_d0, x_d1, out_a, next_b, visit = fence((x_d0, x_d1, out_a, next_b, visit))

    e = jnp.where(inner, next_b, out_a)
    e_x, e_y = along_x(e), along_y(e)
    x_ds0, x_ds1, e_s = fence((core(x_d0), core(x_d1), core(e)))
    x_d = [x_d0, x_d1, x_ds0, x_ds1]
    out_c0, next_c = outward(far_c), across(guest_c)
    (home,) = pair_sums([x], [x_x, x_y, x_xs, x_ys, *x_d], [home], 1024)
    e_x, e_y, out_c0, next_c, home = fence((e_x, e_y, out_c0, next_c, home))

    e_d0, e_d1 = corner(e_x, e_y)
    out_c1 = outward(next_c)
    e_xs, e_ys = fence((core(e_x), core(e_y)))
    lead = 3 * rows - 4 * early
    (visit,) = pair_sums(guest, [*x_d, e, e_s, e_x, e_y, (e_xs, 0, lead)], [visit], 1280)
    e_d0, e_d1, out_c1, visit = fence((e_d0, e_d1, out_c1, visit))

    c = jnp.where(inner, jnp.concatenate([far_c, next_c]), jnp.concatenate([out_c0, out_c1]))
    c_x, c_y = along_x(c), along_y(c)
    e_ds0, e_ds1, c_s = fence((core(e_d0), core(e_d1), core(c)))
    e_d = [e_d0, e_d1, e_ds0, e_ds1]
    visit_0, visit_1 = pair_sums(guest, [(e_xs, lead, early - lead), e_ys, *e_d], [visit], 1024, narrow=True)
    visit_0, visit_1, home = fence((visit_0, visit_1, home))
    back_0 = partner(visit_0)
    (home,) = pair_sums([x], [e, e_s, e_x, e_y, e_xs, e_ys, *e_d], [home], 1280)
    c_x, c_y, back_0, visit_1, home = fence((c_x, c_y, back_0, visit_1, home))

    back_1 = partner(visit_1)
    c_d0, c_d1 = corner(c_x, c_y)
    (home,) = pair_sums([x], [c, c_s, c_x, c_y, core(c_x), core(c_y)], [home], 768)
    c_d0, c_d1, home = fence((c_d0, c_d1, home))
    c_d = [c_d0, c_d1, core(c_d0), core(c_d1)]
    return tuple(pair_sums([x], c_d, [home], 768, back=[back_0, back_1]))


def gram_rows(left, right):
    return lax.dot_general(
        left, right, (((1,), (1,)), ((), ())), preferred_element_type=jnp.float32
    )


def apply_rows(hadam, right):
    return jnp.dot(hadam, right, preferred_element_type=jnp.float32)


def block_terms(lefts, rights):
    grams = [gram_rows(l, r) for l, r in zip(lefts, rights)]
    hadam_a = (grams[1] * grams[2]).astype(jnp.bfloat16)
    hadam_b = (grams[2] * grams[0]).astype(jnp.bfloat16)
    hadam_c = (grams[0] * grams[1]).astype(jnp.bfloat16)
    hadams = (hadam_a, hadam_b, hadam_c)
    return jnp.concatenate([apply_rows(h, r) for h, r in zip(hadams, rights)], axis=1)


def shards(factor_a, factor_b, factor_c):
    own_rows = factor_a.shape[0]
    length = factor_a.shape[1]
    block_j = (
        lax.all_gather(factor_a, "row", axis=0, tiled=True),
        lax.all_gather(factor_b, "row", axis=0, tiled=True),
        lax.all_gather(factor_c, "row", axis=0, tiled=True),
    )
    block_i = (
        lax.all_gather(factor_a, "col", axis=0, tiled=True),
        lax.all_gather(factor_b, "col", axis=0, tiled=True),
        lax.all_gather(factor_c, "col", axis=0, tiled=True),
    )
    lefts = [x for x in block_i]
    summed = lax.psum_scatter(
        block_terms(lefts, block_j).astype(jnp.bfloat16), "col", scatter_dimension=0, tiled=True
    ).astype(jnp.float32)
    cube_a = factor_a.astype(jnp.float32).reshape(own_rows, NMAT, NMAT)
    cube_b = factor_b.astype(jnp.float32).reshape(own_rows, NMAT, NMAT)
    cube_c = factor_c.astype(jnp.float32).reshape(own_rows, NMAT, NMAT)
    data_a = jnp.einsum("rjk,rki->rij", cube_b, cube_c).reshape(own_rows, length)
    data_b = jnp.einsum("rki,rij->rjk", cube_c, cube_a).reshape(own_rows, length)
    data_c = jnp.einsum("rij,rjk->rki", cube_a, cube_b).reshape(own_rows, length)
    grad_a = NMAT * (summed[:, :length] - data_a)
    grad_b = NMAT * (summed[:, length : 2 * length] - data_b)
    grad_c = NMAT * (summed[:, 2 * length :] - data_c)
    return (grad_a, grad_b, grad_c)


def solution(mesh):
    spec = P(("col", "row"), None)
    near = (mesh.shape["row"], mesh.shape["col"]) == (8, 4)
    return jax.shard_map(
        near_shards if near else shards, mesh=mesh, in_specs=(spec,) * 3, out_specs=(spec,) * 3, check_vma=False
    )
```

```python
import functools

import jax
import jax.numpy as jnp
from jax import lax
from jax.experimental import pallas as pl
from jax.experimental.pallas import tpu as pltpu
from jax.sharding import PartitionSpec as P

NMAT = 32
ROW_TILE = 256
LANES = 128
VMEM_BYTES = 63 * 1024 * 1024 + 512 * 1024


def trace_kernel(feat, x_ref, out_ref, left, right, prod):
    blocks = [slice(f * feat, (f + 1) * feat) for f in range(3)]
    for out, (l, r) in enumerate(((1, 2), (2, 0), (0, 1))):
        left[...] = x_ref[:, blocks[l]].astype(jnp.float32).T
        right[...] = x_ref[:, blocks[r]].astype(jnp.float32).T

        def rows(step, carry):
            base = step * 4
            sums = [None] * 4
            for k in range(NMAT):
                line = right[k * NMAT : (k + 1) * NMAT, :]
                for n in range(4):
                    term = left[pl.ds((base + n) * NMAT + k, 1), :] * line
                    sums[n] = term if k == 0 else sums[n] + term
            for n in range(4):
                prod[pl.ds(base + n, NMAT, stride=NMAT), :] = sums[n]
            return carry

        lax.fori_loop(0, NMAT // 4, rows, 0)
        out_ref[:, blocks[out]] = -prod[...].T


def trace_terms(x):
    rows, width = x.shape
    feat = width // 3
    spec = pl.BlockSpec((LANES, width), lambda i: (i, 0))
    return pl.pallas_call(
        functools.partial(trace_kernel, feat),
        grid=(rows // LANES,),
        in_specs=[spec],
        out_specs=spec,
        out_shape=jax.ShapeDtypeStruct((rows, width), jnp.float32),
        scratch_shapes=[pltpu.VMEM((feat, LANES), jnp.float32)] * 3,
        compiler_params=pltpu.CompilerParams(vmem_limit_bytes=VMEM_BYTES),
        cost_estimate=pl.CostEstimate(flops=rows, bytes_accessed=width, transcendentals=0),
    )(x)


def pair_kernel(feat, i_rows, spans, tile, n_sums, narrow, has_y, final, *refs):
    refs = list(refs)
    take = lambda n: [refs.pop(0) for _ in range(n)]
    tiles = sum(count for _, count in spans) // tile
    n_i = sum(i_rows) // ROW_TILE
    per = n_i // n_sums
    blocks = [slice(f * feat, (f + 1) * feat) for f in range(3)]
    i_refs, j_refs = take(len(i_rows)), take(len(spans))
    y_refs = take(n_sums) if has_y else []
    back_ref = take(1)[0] if final else None
    out_refs = take(3 if final else n_sums)
    ibuf, jbuf, acc, i_sem, j_sem, y_sem, o_sem = take(7)
    packed, b_sem = take(2) if narrow or final else (None, None)

    def block(i):
        return pl.ds(i * ROW_TILE, ROW_TILE)

    def fill(buf, sem, sources, ranges, t, size):
        low = 0
        for ref, (first, count) in zip(sources, ranges):
            a, b = max(low, t * size), min(low + count, (t + 1) * size)
            if a < b:
                src = ref.at[pl.ds(first + a - low, b - a)]
                pltpu.make_async_copy(src, buf.at[pl.ds(a, b - a)], sem.at[t]).start()
            low += count

    fill(jbuf, j_sem, j_refs, spans, 0, tile)
    for i in range(n_i):
        fill(ibuf, i_sem, i_refs, [(0, count) for count in i_rows], i, ROW_TILE)
        if has_y:
            pltpu.make_async_copy(y_refs[i // per].at[block(i % per)], acc.at[block(i)], y_sem.at[i]).start()
    for t in range(1, tiles):
        fill(jbuf, j_sem, j_refs, spans, t, tile)
    for i in range(n_i if final else 0):
        pltpu.make_async_copy(back_ref.at[block(i)], packed.at[block(i)], b_sem.at[i]).start()

    def wait(ref, sem):
        pltpu.make_async_copy(ref, ref, sem).wait()

    def over_tiles(t, carry):
        cols = pl.ds(pl.multiple_of(t * tile, tile), tile)
        wait(jbuf.at[cols], j_sem.at[t])

        def over_rows(i, inner):
            span = pl.ds(pl.multiple_of(i * ROW_TILE, ROW_TILE), ROW_TILE)

            @pl.when(t == 0)
            def _():
                wait(ibuf.at[span], i_sem.at[i])

            grams = [
                lax.dot_general(ibuf[span, b], jbuf[cols, b], (((1,), (1,)), ((), ())), preferred_element_type=jnp.float32)
                for b in blocks
            ]
            hadams = [(grams[(f + 1) % 3] * grams[(f + 2) % 3]).astype(jnp.bfloat16) for f in range(3)]

            @pl.when(t == 0)
            def _():
                if has_y:
                    wait(acc.at[span], y_sem.at[i])
                else:
                    acc[span, :] = jnp.zeros((ROW_TILE, 3 * feat), jnp.float32)

            for hadam, b in zip(hadams, blocks):
                acc[span, b] += jnp.dot(hadam, jbuf[cols, b], preferred_element_type=jnp.float32)

            @pl.when(t == tiles - 1)
            def _():
                if final:
                    wait(packed.at[span], b_sem.at[i])
                    acc[span, :] = NMAT * (acc[span, :] + packed[span, :].astype(jnp.float32))
                    for out, b in zip(out_refs, blocks):
                        pltpu.make_async_copy(acc.at[span, b], out.at[span], o_sem.at[i]).start()
                for n in range(0 if final else n_i):
                    @pl.when(i == n)
                    def _():
                        if narrow:
                            packed[block(n), :] = acc[block(n), :].astype(jnp.bfloat16)
                        src = (packed if narrow else acc).at[block(n)]
                        pltpu.make_async_copy(src, out_refs[n // per].at[block(n % per)], o_sem.at[n]).start()
            return inner

        return lax.fori_loop(0, n_i, over_rows, carry)

    lax.fori_loop(0, tiles, over_tiles, 0)
    for i in range(n_i):
        wait((packed if narrow else acc).at[block(i)], o_sem.at[i])


def pair_sums(lefts, rights, sums, tile, narrow=False, back=None):
    width = lefts[0].shape[1]
    feat = width // 3
    i_rows = [v.shape[0] for v in lefts]
    rows = sum(i_rows)
    rights = [r if isinstance(r, tuple) else (r, 0, r.shape[0]) for r in rights]
    spans = [(first, count) for _, first, count in rights]
    total = sum(count for _, count in spans)
    assert total % tile == 0 and rows % ROW_TILE == 0
    n_i = rows // ROW_TILE
    has_y, final = sums is not None, back is not None
    n_sums = len(sums) if has_y else 1
    any_spec = pl.BlockSpec(memory_space=pltpu.HBM)
    operands = [*lefts, *(r for r, _, _ in rights), *(sums or []), *([back] if final else [])]
    first_y = len(lefts) + len(rights)
    if final:
        outs = [jax.ShapeDtypeStruct((rows, feat), jnp.float32)] * 3
    else:
        outs = [jax.ShapeDtypeStruct((rows // n_sums, width), jnp.bfloat16 if narrow else jnp.float32)] * n_sums
    scratch = [
        pltpu.VMEM((rows, width), jnp.bfloat16),
        pltpu.VMEM((total, width), jnp.bfloat16),
        pltpu.VMEM((rows, width), jnp.float32),
        pltpu.SemaphoreType.DMA((n_i,)),
        pltpu.SemaphoreType.DMA((total // tile,)),
        pltpu.SemaphoreType.DMA((n_i,)),
        pltpu.SemaphoreType.DMA((n_i,)),
    ]
    if narrow or final:
        scratch += [pltpu.VMEM((rows, width), jnp.bfloat16), pltpu.SemaphoreType.DMA((n_i,))]
    return pl.pallas_call(
        functools.partial(pair_kernel, feat, i_rows, spans, tile, n_sums, narrow, has_y, final),
        in_specs=[any_spec] * len(operands),
        out_specs=[any_spec] * len(outs),
        out_shape=outs,
        scratch_shapes=scratch,
        input_output_aliases={first_y + n: n for n in range(n_sums)} if has_y and not narrow and not final else {},
        compiler_params=pltpu.CompilerParams(vmem_limit_bytes=VMEM_BYTES),
        cost_estimate=pl.CostEstimate(flops=rows, bytes_accessed=width, transcendentals=0),
    )(*operands)


def cut_kernel(mid, parts, x_ref, y_ref, low_ref, high_ref, low, high, sem):
    size = mid // parts
    spans = [pl.ds(n * size, size) for n in range(parts)]
    moves = []
    for n, span in enumerate(spans):
        moves.append((y_ref.at[span], low.at[span], low_ref.at[span], n))
        moves.append((x_ref.at[pl.ds(mid + n * size, size)], high.at[span], high_ref.at[span], parts + n))
    first = [pltpu.make_async_copy(src, buf, sem.at[0, n]) for src, buf, _, n in moves]
    last = [pltpu.make_async_copy(buf, dst, sem.at[1, n]) for _, buf, dst, n in moves]
    for copy in first:
        copy.start()
    for copy, then in zip(first, last):
        copy.wait()
        then.start()
    for copy in last:
        copy.wait()


def cut(from_x, from_y):
    rows, width = from_x.shape
    mid, parts = rows // 2, 2
    spec = pl.BlockSpec(memory_space=pltpu.HBM)
    return pl.pallas_call(
        functools.partial(cut_kernel, mid, parts),
        in_specs=[spec] * 2,
        out_specs=[spec] * 2,
        out_shape=[jax.ShapeDtypeStruct((mid, width), from_x.dtype)] * 2,
        scratch_shapes=[pltpu.VMEM((mid, width), from_x.dtype)] * 2 + [pltpu.SemaphoreType.DMA((2, 2 * parts))],
        cost_estimate=pl.CostEstimate(flops=0, bytes_accessed=rows * width, transcendentals=0),
    )(from_x, from_y)


def join_kernel(parts, a_ref, b_ref, c_ref, out_ref, low_ref, high_ref, buf, sem):
    rows, feat = a_ref.shape
    size = rows // parts
    spans = [pl.ds(n * size, size) for n in range(parts)]
    loads = [
        [
            pltpu.make_async_copy(ref.at[span], buf.at[span, pl.ds(f * feat, feat)], sem.at[f, n])
            for f, ref in enumerate((a_ref, b_ref, c_ref))
        ]
        for n, span in enumerate(spans)
    ]
    stores = [pltpu.make_async_copy(buf.at[span], out_ref.at[span], sem.at[3, n]) for n, span in enumerate(spans)]
    for copies in loads:
        for copy in copies:
            copy.start()
    for copies, store in zip(loads, stores):
        for copy in copies:
            copy.wait()
        store.start()
    low = low_ref.shape[0]
    stores.append(pltpu.make_async_copy(buf.at[pl.ds(0, low)], low_ref, sem.at[4, 0]))
    stores.append(pltpu.make_async_copy(buf.at[pl.ds(low, rows - low)], high_ref, sem.at[4, 1]))
    for store in stores[-2:]:
        store.start()
    for store in stores:
        store.wait()


def side_by_side(a, b, c, low):
    rows, feat = a.shape
    parts = 4
    spec = pl.BlockSpec(memory_space=pltpu.HBM)
    outs = [jax.ShapeDtypeStruct((n, 3 * feat), a.dtype) for n in (rows, low, rows - low)]
    return pl.pallas_call(
        functools.partial(join_kernel, parts),
        in_specs=[spec] * 3,
        out_specs=[spec] * 3,
        out_shape=outs,
        scratch_shapes=[pltpu.VMEM(outs[0].shape, a.dtype), pltpu.SemaphoreType.DMA((5, parts))],
        cost_estimate=pl.CostEstimate(flops=rows, bytes_accessed=feat, transcendentals=0),
    )(a, b, c)


def near_shards(factor_a, factor_b, factor_c):
    rows = factor_a.shape[0]
    early = rows * 5 // 8
    x, part_a, part_c = side_by_side(factor_a, factor_b, factor_c, early)
    row = lax.axis_index("row")
    inner = (row >= 2) & (row < 6)
    fence = lax.optimization_barrier

    def move(axis, pairs):
        return lambda v: lax.ppermute(v, axis, pairs)

    core = move("row", [(r, r ^ 1) for r in range(8)])
    partner = move("row", [(r, r ^ 2) for r in range(8)])
    across = move("row", [(2, 4), (3, 5), (4, 2), (5, 3)])
    outward = move("row", [(2, 0), (3, 1), (4, 6), (5, 7)])
    along_x = move("col", [(c, c ^ 1) for c in range(4)])
    along_y = move("col", [(c, c ^ 2) for c in range(4)])

    def corner(from_x, from_y):
        low, high = cut(from_x, from_y)
        return along_x(low), along_y(high)

    x_x, x_y, x_s = along_x(x), along_y(x), core(x)
    guest_a, far_a = partner(part_a), across(part_a)
    home = trace_terms(x)
    (home,) = pair_sums([x], [x, x_s], [home], 1024)
    guest_a, far_a, part_c, home = fence((guest_a, far_a, part_c, home))

    guest_c, far_c = partner(part_c), across(part_c)
    x_x, x_y, guest_c, far_c, home = fence((x_x, x_y, guest_c, far_c, home))

    guest = [guest_a, guest_c]
    out_a, next_b = outward(far_a), across(guest_a)
    x_d0, x_d1 = corner(x_x, x_y)
    x_xs, x_ys = fence((core(x_x), core(x_y)))
    (visit,) = pair_sums(guest, [x, x_s, x_x, x_y, x_xs, x_ys], None, 1024)
    x_d0, x_d1, out_a, next_b, visit = fence((x_d0, x_d1, out_a, next_b, visit))

    e = jnp.where(inner, next_b, out_a)
    e_x, e_y = along_x(e), along_y(e)
    x_ds0, x_ds1, e_s = fence((core(x_d0), core(x_d1), core(e)))
    x_d = [x_d0, x_d1, x_ds0, x_ds1]
    out_c0, next_c = outward(far_c), across(guest_c)
    (home,) = pair_sums([x], [x_x, x_y, x_xs, x_ys, *x_d], [home], 1024)
    e_x, e_y, out_c0, next_c, home = fence((e_x, e_y, out_c0, next_c, home))

    e_d0, e_d1 = corner(e_x, e_y)
    out_c1 = outward(next_c)
    e_xs, e_ys = fence((core(e_x), core(e_y)))
    lead = 3 * rows - 4 * early
    (visit,) = pair_sums(guest, [*x_d, e, e_s, e_x, e_y, (e_xs, 0, lead)], [visit], 1280)
    e_d0, e_d1, out_c1, visit = fence((e_d0, e_d1, out_c1, visit))

    c = jnp.where(inner, jnp.concatenate([far_c, next_c]), jnp.concatenate([out_c0, out_c1]))
    c_x, c_y = along_x(c), along_y(c)
    e_ds0, e_ds1, c_s = fence((core(e_d0), core(e_d1), core(c)))
    e_d = [e_d0, e_d1, e_ds0, e_ds1]
    (visit,) = pair_sums(guest, [(e_xs, lead, early - lead), e_ys, *e_d], [visit], 1024, narrow=True)
    visit, home = fence((visit, home))
    back = partner(visit)
    (home,) = pair_sums([x], [e, e_s, e_x, e_y, e_xs, e_ys, *e_d], [home], 1280)
    (home,) = pair_sums([x], [c, c_s], [home], 768)
    c_x, c_y, home = fence((c_x, c_y, home))

    c_d0, c_d1 = corner(c_x, c_y)
    (home,) = pair_sums([x], [c_x, c_y, core(c_x), core(c_y)], [home], 768)
    c_d0, c_d1, back, home = fence((c_d0, c_d1, back, home))
    c_d = [c_d0, c_d1, core(c_d0), core(c_d1)]
    return tuple(pair_sums([x], c_d, [home], 768, back=back))


def gram_rows(left, right):
    return lax.dot_general(
        left, right, (((1,), (1,)), ((), ())), preferred_element_type=jnp.float32
    )


def apply_rows(hadam, right):
    return jnp.dot(hadam, right, preferred_element_type=jnp.float32)


def block_terms(lefts, rights):
    grams = [gram_rows(l, r) for l, r in zip(lefts, rights)]
    hadam_a = (grams[1] * grams[2]).astype(jnp.bfloat16)
    hadam_b = (grams[2] * grams[0]).astype(jnp.bfloat16)
    hadam_c = (grams[0] * grams[1]).astype(jnp.bfloat16)
    hadams = (hadam_a, hadam_b, hadam_c)
    return jnp.concatenate([apply_rows(h, r) for h, r in zip(hadams, rights)], axis=1)


def shards(factor_a, factor_b, factor_c):
    own_rows = factor_a.shape[0]
    length = factor_a.shape[1]
    block_j = (
        lax.all_gather(factor_a, "row", axis=0, tiled=True),
        lax.all_gather(factor_b, "row", axis=0, tiled=True),
        lax.all_gather(factor_c, "row", axis=0, tiled=True),
    )
    block_i = (
        lax.all_gather(factor_a, "col", axis=0, tiled=True),
        lax.all_gather(factor_b, "col", axis=0, tiled=True),
        lax.all_gather(factor_c, "col", axis=0, tiled=True),
    )
    lefts = [x for x in block_i]
    summed = lax.psum_scatter(
        block_terms(lefts, block_j).astype(jnp.bfloat16), "col", scatter_dimension=0, tiled=True
    ).astype(jnp.float32)
    cube_a = factor_a.astype(jnp.float32).reshape(own_rows, NMAT, NMAT)
    cube_b = factor_b.astype(jnp.float32).reshape(own_rows, NMAT, NMAT)
    cube_c = factor_c.astype(jnp.float32).reshape(own_rows, NMAT, NMAT)
    data_a = jnp.einsum("rjk,rki->rij", cube_b, cube_c).reshape(own_rows, length)
    data_b = jnp.einsum("rki,rij->rjk", cube_c, cube_a).reshape(own_rows, length)
    data_c = jnp.einsum("rij,rjk->rki", cube_a, cube_b).reshape(own_rows, length)
    grad_a = NMAT * (summed[:, :length] - data_a)
    grad_b = NMAT * (summed[:, length : 2 * length] - data_b)
    grad_c = NMAT * (summed[:, 2 * length :] - data_c)
    return (grad_a, grad_b, grad_c)


def solution(mesh):
    spec = P(("col", "row"), None)
    near = (mesh.shape["row"], mesh.shape["col"]) == (8, 4)
    return jax.shard_map(
        near_shards if near else shards, mesh=mesh, in_specs=(spec,) * 3, out_specs=(spec,) * 3, check_vma=False
    )
```

```python
import functools

import jax
import jax.numpy as jnp
from jax import lax
from jax.experimental import pallas as pl
from jax.experimental.pallas import tpu as pltpu
from jax.sharding import PartitionSpec as P

NMAT = 32
ROW_TILE = 256
LANES = 128
VMEM_BYTES = 63 * 1024 * 1024 + 512 * 1024


def trace_kernel(feat, x_ref, out_ref, left, right, prod):
    blocks = [slice(f * feat, (f + 1) * feat) for f in range(3)]
    for out, (l, r) in enumerate(((1, 2), (2, 0), (0, 1))):
        left[...] = x_ref[:, blocks[l]].astype(jnp.float32).T
        right[...] = x_ref[:, blocks[r]].astype(jnp.float32).T

        def rows(step, carry):
            base = step * 4
            sums = [None] * 4
            for k in range(NMAT):
                line = right[k * NMAT : (k + 1) * NMAT, :]
                for n in range(4):
                    term = left[pl.ds((base + n) * NMAT + k, 1), :] * line
                    sums[n] = term if k == 0 else sums[n] + term
            for n in range(4):
                prod[pl.ds(base + n, NMAT, stride=NMAT), :] = sums[n]
            return carry

        lax.fori_loop(0, NMAT // 4, rows, 0)
        out_ref[:, blocks[out]] = -prod[...].T


def trace_terms(x):
    rows, width = x.shape
    feat = width // 3
    spec = pl.BlockSpec((LANES, width), lambda i: (i, 0))
    return pl.pallas_call(
        functools.partial(trace_kernel, feat),
        grid=(rows // LANES,),
        in_specs=[spec],
        out_specs=spec,
        out_shape=jax.ShapeDtypeStruct((rows, width), jnp.float32),
        scratch_shapes=[pltpu.VMEM((feat, LANES), jnp.float32)] * 3,
        compiler_params=pltpu.CompilerParams(vmem_limit_bytes=VMEM_BYTES),
        cost_estimate=pl.CostEstimate(flops=rows, bytes_accessed=width, transcendentals=0),
    )(x)


def pair_kernel(feat, i_rows, spans, tile, n_sums, narrow, has_y, final, *refs):
    refs = list(refs)
    take = lambda n: [refs.pop(0) for _ in range(n)]
    tiles = sum(count for _, count in spans) // tile
    n_i = sum(i_rows) // ROW_TILE
    per = n_i // n_sums
    blocks = [slice(f * feat, (f + 1) * feat) for f in range(3)]
    i_refs, j_refs = take(len(i_rows)), take(len(spans))
    y_refs = take(n_sums) if has_y else []
    back_ref = take(1)[0] if final else None
    out_refs = take(3 if final else n_sums)
    ibuf, jbuf, acc, i_sem, j_sem, y_sem, o_sem = take(7)
    packed, b_sem = take(2) if narrow or final else (None, None)

    def block(i):
        return pl.ds(i * ROW_TILE, ROW_TILE)

    def fill(buf, sem, sources, ranges, t, size):
        low = 0
        for ref, (first, count) in zip(sources, ranges):
            a, b = max(low, t * size), min(low + count, (t + 1) * size)
            if a < b:
                src = ref.at[pl.ds(first + a - low, b - a)]
                pltpu.make_async_copy(src, buf.at[pl.ds(a, b - a)], sem.at[t]).start()
            low += count

    fill(jbuf, j_sem, j_refs, spans, 0, tile)
    for i in range(n_i):
        fill(ibuf, i_sem, i_refs, [(0, count) for count in i_rows], i, ROW_TILE)
        if has_y:
            pltpu.make_async_copy(y_refs[i // per].at[block(i % per)], acc.at[block(i)], y_sem.at[i]).start()
    for t in range(1, tiles):
        fill(jbuf, j_sem, j_refs, spans, t, tile)
    for i in range(n_i if final else 0):
        pltpu.make_async_copy(back_ref.at[block(i)], packed.at[block(i)], b_sem.at[i]).start()

    def wait(ref, sem):
        pltpu.make_async_copy(ref, ref, sem).wait()

    def over_tiles(t, carry):
        cols = pl.ds(pl.multiple_of(t * tile, tile), tile)
        wait(jbuf.at[cols], j_sem.at[t])

        def over_rows(i, inner):
            span = pl.ds(pl.multiple_of(i * ROW_TILE, ROW_TILE), ROW_TILE)

            @pl.when(t == 0)
            def _():
                wait(ibuf.at[span], i_sem.at[i])

            grams = [
                lax.dot_general(ibuf[span, b], jbuf[cols, b], (((1,), (1,)), ((), ())), preferred_element_type=jnp.float32)
                for b in blocks
            ]
            hadams = [(grams[(f + 1) % 3] * grams[(f + 2) % 3]).astype(jnp.bfloat16) for f in range(3)]

            @pl.when(t == 0)
            def _():
                if has_y:
                    wait(acc.at[span], y_sem.at[i])
                else:
                    acc[span, :] = jnp.zeros((ROW_TILE, 3 * feat), jnp.float32)

            for hadam, b in zip(hadams, blocks):
                acc[span, b] += jnp.dot(hadam, jbuf[cols, b], preferred_element_type=jnp.float32)

            @pl.when(t == tiles - 1)
            def _():
                if final:
                    wait(packed.at[span], b_sem.at[i])
                    acc[span, :] = NMAT * (acc[span, :] + packed[span, :].astype(jnp.float32))
                    for out, b in zip(out_refs, blocks):
                        pltpu.make_async_copy(acc.at[span, b], out.at[span], o_sem.at[i]).start()
                for n in range(0 if final else n_i):
                    @pl.when(i == n)
                    def _():
                        if narrow:
                            packed[block(n), :] = acc[block(n), :].astype(jnp.bfloat16)
                        src = (packed if narrow else acc).at[block(n)]
                        pltpu.make_async_copy(src, out_refs[n // per].at[block(n % per)], o_sem.at[n]).start()
            return inner

        return lax.fori_loop(0, n_i, over_rows, carry)

    lax.fori_loop(0, tiles, over_tiles, 0)
    for i in range(n_i):
        wait((packed if narrow else acc).at[block(i)], o_sem.at[i])


def pair_sums(lefts, rights, sums, tile, narrow=False, back=None):
    width = lefts[0].shape[1]
    feat = width // 3
    i_rows = [v.shape[0] for v in lefts]
    rows = sum(i_rows)
    rights = [r if isinstance(r, tuple) else (r, 0, r.shape[0]) for r in rights]
    spans = [(first, count) for _, first, count in rights]
    total = sum(count for _, count in spans)
    assert total % tile == 0 and rows % ROW_TILE == 0
    n_i = rows // ROW_TILE
    has_y, final = sums is not None, back is not None
    n_sums = len(sums) if has_y else 1
    any_spec = pl.BlockSpec(memory_space=pltpu.HBM)
    operands = [*lefts, *(r for r, _, _ in rights), *(sums or []), *([back] if final else [])]
    first_y = len(lefts) + len(rights)
    if final:
        outs = [jax.ShapeDtypeStruct((rows, feat), jnp.float32)] * 3
    else:
        outs = [jax.ShapeDtypeStruct((rows // n_sums, width), jnp.bfloat16 if narrow else jnp.float32)] * n_sums
    scratch = [
        pltpu.VMEM((rows, width), jnp.bfloat16),
        pltpu.VMEM((total, width), jnp.bfloat16),
        pltpu.VMEM((rows, width), jnp.float32),
        pltpu.SemaphoreType.DMA((n_i,)),
        pltpu.SemaphoreType.DMA((total // tile,)),
        pltpu.SemaphoreType.DMA((n_i,)),
        pltpu.SemaphoreType.DMA((n_i,)),
    ]
    if narrow or final:
        scratch += [pltpu.VMEM((rows, width), jnp.bfloat16), pltpu.SemaphoreType.DMA((n_i,))]
    return pl.pallas_call(
        functools.partial(pair_kernel, feat, i_rows, spans, tile, n_sums, narrow, has_y, final),
        in_specs=[any_spec] * len(operands),
        out_specs=[any_spec] * len(outs),
        out_shape=outs,
        scratch_shapes=scratch,
        input_output_aliases={first_y + n: n for n in range(n_sums)} if has_y and not narrow and not final else {},
        compiler_params=pltpu.CompilerParams(vmem_limit_bytes=VMEM_BYTES),
        cost_estimate=pl.CostEstimate(flops=rows, bytes_accessed=width, transcendentals=0),
    )(*operands)


def cut_kernel(mid, parts, x_ref, y_ref, low_ref, high_ref, low, high, sem):
    size = mid // parts
    spans = [pl.ds(n * size, size) for n in range(parts)]
    moves = []
    for n, span in enumerate(spans):
        moves.append((y_ref.at[span], low.at[span], low_ref.at[span], n))
        moves.append((x_ref.at[pl.ds(mid + n * size, size)], high.at[span], high_ref.at[span], parts + n))
    first = [pltpu.make_async_copy(src, buf, sem.at[0, n]) for src, buf, _, n in moves]
    last = [pltpu.make_async_copy(buf, dst, sem.at[1, n]) for _, buf, dst, n in moves]
    for copy in first:
        copy.start()
    for copy, then in zip(first, last):
        copy.wait()
        then.start()
    for copy in last:
        copy.wait()


def cut(from_x, from_y):
    rows, width = from_x.shape
    mid, parts = rows // 2, 2
    spec = pl.BlockSpec(memory_space=pltpu.HBM)
    return pl.pallas_call(
        functools.partial(cut_kernel, mid, parts),
        in_specs=[spec] * 2,
        out_specs=[spec] * 2,
        out_shape=[jax.ShapeDtypeStruct((mid, width), from_x.dtype)] * 2,
        scratch_shapes=[pltpu.VMEM((mid, width), from_x.dtype)] * 2 + [pltpu.SemaphoreType.DMA((2, 2 * parts))],
        cost_estimate=pl.CostEstimate(flops=0, bytes_accessed=rows * width, transcendentals=0),
    )(from_x, from_y)


def join_kernel(parts, a_ref, b_ref, c_ref, out_ref, low_ref, high_ref, buf, sem):
    rows, feat = a_ref.shape
    size = rows // parts
    spans = [pl.ds(n * size, size) for n in range(parts)]
    loads = [
        [
            pltpu.make_async_copy(ref.at[span], buf.at[span, pl.ds(f * feat, feat)], sem.at[f, n])
            for f, ref in enumerate((a_ref, b_ref, c_ref))
        ]
        for n, span in enumerate(spans)
    ]
    stores = [pltpu.make_async_copy(buf.at[span], out_ref.at[span], sem.at[3, n]) for n, span in enumerate(spans)]
    for copies in loads:
        for copy in copies:
            copy.start()
    for copies, store in zip(loads, stores):
        for copy in copies:
            copy.wait()
        store.start()
    low = low_ref.shape[0]
    stores.append(pltpu.make_async_copy(buf.at[pl.ds(0, low)], low_ref, sem.at[4, 0]))
    stores.append(pltpu.make_async_copy(buf.at[pl.ds(low, rows - low)], high_ref, sem.at[4, 1]))
    for store in stores[-2:]:
        store.start()
    for store in stores:
        store.wait()


def side_by_side(a, b, c, low):
    rows, feat = a.shape
    parts = 4
    spec = pl.BlockSpec(memory_space=pltpu.HBM)
    outs = [jax.ShapeDtypeStruct((n, 3 * feat), a.dtype) for n in (rows, low, rows - low)]
    return pl.pallas_call(
        functools.partial(join_kernel, parts),
        in_specs=[spec] * 3,
        out_specs=[spec] * 3,
        out_shape=outs,
        scratch_shapes=[pltpu.VMEM(outs[0].shape, a.dtype), pltpu.SemaphoreType.DMA((5, parts))],
        cost_estimate=pl.CostEstimate(flops=rows, bytes_accessed=feat, transcendentals=0),
    )(a, b, c)


def near_shards(factor_a, factor_b, factor_c):
    rows = factor_a.shape[0]
    early = rows * 5 // 8
    x, part_a, part_c = side_by_side(factor_a, factor_b, factor_c, early)
    row = lax.axis_index("row")
    inner = (row >= 2) & (row < 6)
    fence = lax.optimization_barrier

    def move(axis, pairs):
        return lambda v: lax.ppermute(v, axis, pairs)

    core = move("row", [(r, r ^ 1) for r in range(8)])
    partner = move("row", [(r, r ^ 2) for r in range(8)])
    across = move("row", [(2, 4), (3, 5), (4, 2), (5, 3)])
    outward = move("row", [(2, 0), (3, 1), (4, 6), (5, 7)])
    along_x = move("col", [(c, c ^ 1) for c in range(4)])
    along_y = move("col", [(c, c ^ 2) for c in range(4)])

    def corner(from_x, from_y):
        low, high = cut(from_x, from_y)
        return along_x(low), along_y(high)

    x_x, x_y, x_s = along_x(x), along_y(x), core(x)
    guest_a, far_a = partner(part_a), across(part_a)
    home = trace_terms(x)
    (home,) = pair_sums([x], [x, x_s], [home], 1024)
    guest_a, far_a, part_c, home = fence((guest_a, far_a, part_c, home))

    guest_c, far_c = partner(part_c), across(part_c)
    x_x, x_y, guest_c, far_c, home = fence((x_x, x_y, guest_c, far_c, home))

    guest = [guest_a, guest_c]
    out_a, next_b = outward(far_a), across(guest_a)
    x_d0, x_d1 = corner(x_x, x_y)
    x_xs, x_ys = fence((core(x_x), core(x_y)))
    (visit,) = pair_sums(guest, [x, x_s, x_x, x_y, x_xs, x_ys], None, 1024)
    x_d0, x_d1, out_a, next_b, visit = fence((x_d0, x_d1, out_a, next_b, visit))

    e = jnp.where(inner, next_b, out_a)
    e_x, e_y = along_x(e), along_y(e)
    x_ds0, x_ds1, e_s = fence((core(x_d0), core(x_d1), core(e)))
    x_d = [x_d0, x_d1, x_ds0, x_ds1]
    out_c0, next_c = outward(far_c), across(guest_c)
    ahead = rows - early
    (home,) = pair_sums([x], [x_x, x_y, x_xs, x_ys, *x_d, e, (e_s, 0, ahead)], [home], 1792)
    e_x, e_y, out_c0, next_c, home = fence((e_x, e_y, out_c0, next_c, home))

    e_d0, e_d1 = corner(e_x, e_y)
    out_c1 = outward(next_c)
    e_xs, e_ys = fence((core(e_x), core(e_y)))
    lead = 3 * rows - 4 * early
    (visit,) = pair_sums(guest, [*x_d, e, e_s, e_x, e_y, (e_xs, 0, lead)], [visit], 1280)
    e_d0, e_d1, out_c1, visit = fence((e_d0, e_d1, out_c1, visit))

    c = jnp.where(inner, jnp.concatenate([far_c, next_c]), jnp.concatenate([out_c0, out_c1]))
    c_x, c_y = along_x(c), along_y(c)
    e_ds0, e_ds1 = fence((core(e_d0), core(e_d1)))
    c_s = core(c)
    e_d = [e_d0, e_d1, e_ds0, e_ds1]
    (visit,) = pair_sums(guest, [(e_xs, lead, early - lead), e_ys, *e_d], [visit], 1024, narrow=True)
    visit, home = fence((visit, home))
    back = partner(visit)
    (home,) = pair_sums([x], [(e_s, ahead, early - ahead), e_x, e_y, e_xs, e_ys, *e_d], [home], 1024)
    (home,) = pair_sums([x], [c, c_s], [home], 768)
    c_x, c_y, home = fence((c_x, c_y, home))

    c_d0, c_d1 = corner(c_x, c_y)
    (home,) = pair_sums([x], [c_x, c_y, core(c_x), core(c_y)], [home], 768)
    c_d0, c_d1, back, home = fence((c_d0, c_d1, back, home))
    c_d = [c_d0, c_d1, core(c_d0), core(c_d1)]
    return tuple(pair_sums([x], c_d, [home], 768, back=back))


def gram_rows(left, right):
    return lax.dot_general(
        left, right, (((1,), (1,)), ((), ())), preferred_element_type=jnp.float32
    )


def apply_rows(hadam, right):
    return jnp.dot(hadam, right, preferred_element_type=jnp.float32)


def block_terms(lefts, rights):
    grams = [gram_rows(l, r) for l, r in zip(lefts, rights)]
    hadam_a = (grams[1] * grams[2]).astype(jnp.bfloat16)
    hadam_b = (grams[2] * grams[0]).astype(jnp.bfloat16)
    hadam_c = (grams[0] * grams[1]).astype(jnp.bfloat16)
    hadams = (hadam_a, hadam_b, hadam_c)
    return jnp.concatenate([apply_rows(h, r) for h, r in zip(hadams, rights)], axis=1)


def shards(factor_a, factor_b, factor_c):
    own_rows = factor_a.shape[0]
    length = factor_a.shape[1]
    block_j = (
        lax.all_gather(factor_a, "row", axis=0, tiled=True),
        lax.all_gather(factor_b, "row", axis=0, tiled=True),
        lax.all_gather(factor_c, "row", axis=0, tiled=True),
    )
    block_i = (
        lax.all_gather(factor_a, "col", axis=0, tiled=True),
        lax.all_gather(factor_b, "col", axis=0, tiled=True),
        lax.all_gather(factor_c, "col", axis=0, tiled=True),
    )
    lefts = [x for x in block_i]
    summed = lax.psum_scatter(
        block_terms(lefts, block_j).astype(jnp.bfloat16), "col", scatter_dimension=0, tiled=True
    ).astype(jnp.float32)
    cube_a = factor_a.astype(jnp.float32).reshape(own_rows, NMAT, NMAT)
    cube_b = factor_b.astype(jnp.float32).reshape(own_rows, NMAT, NMAT)
    cube_c = factor_c.astype(jnp.float32).reshape(own_rows, NMAT, NMAT)
    data_a = jnp.einsum("rjk,rki->rij", cube_b, cube_c).reshape(own_rows, length)
    data_b = jnp.einsum("rki,rij->rjk", cube_c, cube_a).reshape(own_rows, length)
    data_c = jnp.einsum("rij,rjk->rki", cube_a, cube_b).reshape(own_rows, length)
    grad_a = NMAT * (summed[:, :length] - data_a)
    grad_b = NMAT * (summed[:, length : 2 * length] - data_b)
    grad_c = NMAT * (summed[:, 2 * length :] - data_c)
    return (grad_a, grad_b, grad_c)


def solution(mesh):
    spec = P(("col", "row"), None)
    near = (mesh.shape["row"], mesh.shape["col"]) == (8, 4)
    return jax.shard_map(
        near_shards if near else shards, mesh=mesh, in_specs=(spec,) * 3, out_specs=(spec,) * 3, check_vma=False
    )
```

```python
import functools

import jax
import jax.numpy as jnp
from jax import lax
from jax.experimental import pallas as pl
from jax.experimental.pallas import tpu as pltpu
from jax.sharding import PartitionSpec as P

NMAT = 32
ROW_TILE = 256
LANES = 128
VMEM_BYTES = 63 * 1024 * 1024 + 512 * 1024


def trace_kernel(feat, x_ref, out_ref, left, right, prod):
    blocks = [slice(f * feat, (f + 1) * feat) for f in range(3)]
    for out, (l, r) in enumerate(((1, 2), (2, 0), (0, 1))):
        left[...] = x_ref[:, blocks[l]].astype(jnp.float32).T
        right[...] = x_ref[:, blocks[r]].astype(jnp.float32).T

        def rows(step, carry):
            base = step * 4
            sums = [None] * 4
            for k in range(NMAT):
                line = right[k * NMAT : (k + 1) * NMAT, :]
                for n in range(4):
                    term = left[pl.ds((base + n) * NMAT + k, 1), :] * line
                    sums[n] = term if k == 0 else sums[n] + term
            for n in range(4):
                prod[pl.ds(base + n, NMAT, stride=NMAT), :] = sums[n]
            return carry

        lax.fori_loop(0, NMAT // 4, rows, 0)
        out_ref[:, blocks[out]] = -prod[...].T


def trace_terms(x):
    rows, width = x.shape
    feat = width // 3
    spec = pl.BlockSpec((LANES, width), lambda i: (i, 0))
    return pl.pallas_call(
        functools.partial(trace_kernel, feat),
        grid=(rows // LANES,),
        in_specs=[spec],
        out_specs=spec,
        out_shape=jax.ShapeDtypeStruct((rows, width), jnp.float32),
        scratch_shapes=[pltpu.VMEM((feat, LANES), jnp.float32)] * 3,
        compiler_params=pltpu.CompilerParams(vmem_limit_bytes=VMEM_BYTES),
        cost_estimate=pl.CostEstimate(flops=rows, bytes_accessed=width, transcendentals=0),
    )(x)


def pair_kernel(feat, i_rows, spans, tile, n_sums, narrow, has_y, final, *refs):
    refs = list(refs)
    take = lambda n: [refs.pop(0) for _ in range(n)]
    tiles = sum(count for _, count in spans) // tile
    n_i = sum(i_rows) // ROW_TILE
    per = n_i // n_sums
    blocks = [slice(f * feat, (f + 1) * feat) for f in range(3)]
    i_refs, j_refs = take(len(i_rows)), take(len(spans))
    y_refs = take(n_sums) if has_y else []
    back_ref = take(1)[0] if final else None
    out_refs = take(3 if final else n_sums)
    ibuf, jbuf, acc, i_sem, j_sem, y_sem, o_sem = take(7)
    packed, b_sem = take(2) if narrow or final else (None, None)

    def block(i):
        return pl.ds(i * ROW_TILE, ROW_TILE)

    def fill(buf, sem, sources, ranges, t, size):
        low = 0
        for ref, (first, count) in zip(sources, ranges):
            a, b = max(low, t * size), min(low + count, (t + 1) * size)
            if a < b:
                src = ref.at[pl.ds(first + a - low, b - a)]
                pltpu.make_async_copy(src, buf.at[pl.ds(a, b - a)], sem.at[t]).start()
            low += count

    fill(jbuf, j_sem, j_refs, spans, 0, tile)
    for i in range(n_i):
        fill(ibuf, i_sem, i_refs, [(0, count) for count in i_rows], i, ROW_TILE)
        if has_y:
            pltpu.make_async_copy(y_refs[i // per].at[block(i % per)], acc.at[block(i)], y_sem.at[i]).start()
    for t in range(1, tiles):
        fill(jbuf, j_sem, j_refs, spans, t, tile)
    for i in range(n_i if final else 0):
        pltpu.make_async_copy(back_ref.at[block(i)], packed.at[block(i)], b_sem.at[i]).start()

    def wait(ref, sem):
        pltpu.make_async_copy(ref, ref, sem).wait()

    def over_tiles(t, carry):
        cols = pl.ds(pl.multiple_of(t * tile, tile), tile)
        wait(jbuf.at[cols], j_sem.at[t])

        def over_rows(i, inner):
            span = pl.ds(pl.multiple_of(i * ROW_TILE, ROW_TILE), ROW_TILE)

            @pl.when(t == 0)
            def _():
                wait(ibuf.at[span], i_sem.at[i])

            grams = [
                lax.dot_general(ibuf[span, b], jbuf[cols, b], (((1,), (1,)), ((), ())), preferred_element_type=jnp.float32)
                for b in blocks
            ]
            hadams = [(grams[(f + 1) % 3] * grams[(f + 2) % 3]).astype(jnp.bfloat16) for f in range(3)]

            @pl.when(t == 0)
            def _():
                if has_y:
                    wait(acc.at[span], y_sem.at[i])
                else:
                    acc[span, :] = jnp.zeros((ROW_TILE, 3 * feat), jnp.float32)

            for hadam, b in zip(hadams, blocks):
                acc[span, b] += jnp.dot(hadam, jbuf[cols, b], preferred_element_type=jnp.float32)

            @pl.when(t == tiles - 1)
            def _():
                if final:
                    wait(packed.at[span], b_sem.at[i])
                    acc[span, :] = NMAT * (acc[span, :] + packed[span, :].astype(jnp.float32))
                    for out, b in zip(out_refs, blocks):
                        pltpu.make_async_copy(acc.at[span, b], out.at[span], o_sem.at[i]).start()
                for n in range(0 if final else n_i):
                    @pl.when(i == n)
                    def _():
                        if narrow:
                            packed[block(n), :] = acc[block(n), :].astype(jnp.bfloat16)
                        src = (packed if narrow else acc).at[block(n)]
                        pltpu.make_async_copy(src, out_refs[n // per].at[block(n % per)], o_sem.at[n]).start()
            return inner

        return lax.fori_loop(0, n_i, over_rows, carry)

    lax.fori_loop(0, tiles, over_tiles, 0)
    for i in range(n_i):
        wait((packed if narrow else acc).at[block(i)], o_sem.at[i])


def pair_sums(lefts, rights, sums, tile, narrow=False, back=None):
    width = lefts[0].shape[1]
    feat = width // 3
    i_rows = [v.shape[0] for v in lefts]
    rows = sum(i_rows)
    rights = [r if isinstance(r, tuple) else (r, 0, r.shape[0]) for r in rights]
    spans = [(first, count) for _, first, count in rights]
    total = sum(count for _, count in spans)
    assert total % tile == 0 and rows % ROW_TILE == 0
    n_i = rows // ROW_TILE
    has_y, final = sums is not None, back is not None
    n_sums = len(sums) if has_y else 1
    any_spec = pl.BlockSpec(memory_space=pltpu.HBM)
    operands = [*lefts, *(r for r, _, _ in rights), *(sums or []), *([back] if final else [])]
    first_y = len(lefts) + len(rights)
    if final:
        outs = [jax.ShapeDtypeStruct((rows, feat), jnp.float32)] * 3
    else:
        outs = [jax.ShapeDtypeStruct((rows // n_sums, width), jnp.bfloat16 if narrow else jnp.float32)] * n_sums
    scratch = [
        pltpu.VMEM((rows, width), jnp.bfloat16),
        pltpu.VMEM((total, width), jnp.bfloat16),
        pltpu.VMEM((rows, width), jnp.float32),
        pltpu.SemaphoreType.DMA((n_i,)),
        pltpu.SemaphoreType.DMA((total // tile,)),
        pltpu.SemaphoreType.DMA((n_i,)),
        pltpu.SemaphoreType.DMA((n_i,)),
    ]
    if narrow or final:
        scratch += [pltpu.VMEM((rows, width), jnp.bfloat16), pltpu.SemaphoreType.DMA((n_i,))]
    return pl.pallas_call(
        functools.partial(pair_kernel, feat, i_rows, spans, tile, n_sums, narrow, has_y, final),
        in_specs=[any_spec] * len(operands),
        out_specs=[any_spec] * len(outs),
        out_shape=outs,
        scratch_shapes=scratch,
        input_output_aliases={first_y + n: n for n in range(n_sums)} if has_y and not narrow and not final else {},
        compiler_params=pltpu.CompilerParams(vmem_limit_bytes=VMEM_BYTES),
        cost_estimate=pl.CostEstimate(flops=rows, bytes_accessed=width, transcendentals=0),
    )(*operands)


def cut_kernel(mid, parts, x_ref, y_ref, low_ref, high_ref, low, high, sem):
    size = mid // parts
    spans = [pl.ds(n * size, size) for n in range(parts)]
    moves = []
    for n, span in enumerate(spans):
        moves.append((y_ref.at[span], low.at[span], low_ref.at[span], n))
        moves.append((x_ref.at[pl.ds(mid + n * size, size)], high.at[span], high_ref.at[span], parts + n))
    first = [pltpu.make_async_copy(src, buf, sem.at[0, n]) for src, buf, _, n in moves]
    last = [pltpu.make_async_copy(buf, dst, sem.at[1, n]) for _, buf, dst, n in moves]
    for copy in first:
        copy.start()
    for copy, then in zip(first, last):
        copy.wait()
        then.start()
    for copy in last:
        copy.wait()


def cut(from_x, from_y):
    rows, width = from_x.shape
    mid, parts = rows // 2, 2
    spec = pl.BlockSpec(memory_space=pltpu.HBM)
    return pl.pallas_call(
        functools.partial(cut_kernel, mid, parts),
        in_specs=[spec] * 2,
        out_specs=[spec] * 2,
        out_shape=[jax.ShapeDtypeStruct((mid, width), from_x.dtype)] * 2,
        scratch_shapes=[pltpu.VMEM((mid, width), from_x.dtype)] * 2 + [pltpu.SemaphoreType.DMA((2, 2 * parts))],
        cost_estimate=pl.CostEstimate(flops=0, bytes_accessed=rows * width, transcendentals=0),
    )(from_x, from_y)


def join_kernel(parts, a_ref, b_ref, c_ref, out_ref, low_ref, high_ref, buf, sem):
    rows, feat = a_ref.shape
    size = rows // parts
    spans = [pl.ds(n * size, size) for n in range(parts)]
    loads = [
        [
            pltpu.make_async_copy(ref.at[span], buf.at[span, pl.ds(f * feat, feat)], sem.at[f, n])
            for f, ref in enumerate((a_ref, b_ref, c_ref))
        ]
        for n, span in enumerate(spans)
    ]
    stores = [pltpu.make_async_copy(buf.at[span], out_ref.at[span], sem.at[3, n]) for n, span in enumerate(spans)]
    for copies in loads:
        for copy in copies:
            copy.start()
    for copies, store in zip(loads, stores):
        for copy in copies:
            copy.wait()
        store.start()
    low = low_ref.shape[0]
    stores.append(pltpu.make_async_copy(buf.at[pl.ds(0, low)], low_ref, sem.at[4, 0]))
    stores.append(pltpu.make_async_copy(buf.at[pl.ds(low, rows - low)], high_ref, sem.at[4, 1]))
    for store in stores[-2:]:
        store.start()
    for store in stores:
        store.wait()


def side_by_side(a, b, c, low):
    rows, feat = a.shape
    parts = 4
    spec = pl.BlockSpec(memory_space=pltpu.HBM)
    outs = [jax.ShapeDtypeStruct((n, 3 * feat), a.dtype) for n in (rows, low, rows - low)]
    return pl.pallas_call(
        functools.partial(join_kernel, parts),
        in_specs=[spec] * 3,
        out_specs=[spec] * 3,
        out_shape=outs,
        scratch_shapes=[pltpu.VMEM(outs[0].shape, a.dtype), pltpu.SemaphoreType.DMA((5, parts))],
        cost_estimate=pl.CostEstimate(flops=rows, bytes_accessed=feat, transcendentals=0),
    )(a, b, c)


def near_shards(factor_a, factor_b, factor_c):
    rows = factor_a.shape[0]
    early = rows * 5 // 8
    x, part_a, part_c = side_by_side(factor_a, factor_b, factor_c, early)
    row = lax.axis_index("row")
    inner = (row >= 2) & (row < 6)
    fence = lax.optimization_barrier

    def move(axis, pairs):
        return lambda v: lax.ppermute(v, axis, pairs)

    core = move("row", [(r, r ^ 1) for r in range(8)])
    partner = move("row", [(r, r ^ 2) for r in range(8)])
    across = move("row", [(2, 4), (3, 5), (4, 2), (5, 3)])
    outward = move("row", [(2, 0), (3, 1), (4, 6), (5, 7)])
    along_x = move("col", [(c, c ^ 1) for c in range(4)])
    along_y = move("col", [(c, c ^ 2) for c in range(4)])

    def corner(from_x, from_y):
        low, high = cut(from_x, from_y)
        return along_x(low), along_y(high)

    x_x, x_y, x_s = along_x(x), along_y(x), core(x)
    guest_a, far_a = partner(part_a), across(part_a)
    home = trace_terms(x)
    (home,) = pair_sums([x], [x, x_s], [home], 1024)
    guest_a, far_a, part_c, home = fence((guest_a, far_a, part_c, home))

    guest_c, far_c = partner(part_c), across(part_c)
    x_x, x_y, guest_c, far_c, home = fence((x_x, x_y, guest_c, far_c, home))

    guest = [guest_a, guest_c]
    out_a, next_b = outward(far_a), across(guest_a)
    x_d0, x_d1 = corner(x_x, x_y)
    x_xs, x_ys = fence((core(x_x), core(x_y)))
    (visit,) = pair_sums(guest, [x, x_s, x_x, x_y, x_xs, x_ys], None, 1024)
    x_d0, x_d1, out_a, next_b, visit = fence((x_d0, x_d1, out_a, next_b, visit))

    e = jnp.where(inner, next_b, out_a)
    e_x, e_y = along_x(e), along_y(e)
    x_ds0, x_ds1, e_s = fence((core(x_d0), core(x_d1), core(e)))
    x_d = [x_d0, x_d1, x_ds0, x_ds1]
    out_c0, next_c = outward(far_c), across(guest_c)
    ahead = rows - early
    (home,) = pair_sums([x], [x_x, x_y, x_xs, x_ys, *x_d, e, (e_s, 0, ahead)], [home], 1792)
    e_x, e_y, out_c0, next_c, home = fence((e_x, e_y, out_c0, next_c, home))

    e_d0, e_d1 = corner(e_x, e_y)
    out_c1 = outward(next_c)
    e_xs, e_ys = fence((core(e_x), core(e_y)))
    lead = 3 * rows - 4 * early
    (visit,) = pair_sums(guest, [*x_d, e, e_s, e_x, e_y, (e_xs, 0, lead)], [visit], 1280)
    e_d0, e_d1, out_c1, visit = fence((e_d0, e_d1, out_c1, visit))

    c = jnp.where(inner, jnp.concatenate([far_c, next_c]), jnp.concatenate([out_c0, out_c1]))
    c, e_ds0, e_ds1 = fence((c, core(e_d0), core(e_d1)))
    c_x, c_y, c_s = along_x(c), along_y(c), core(c)
    e_d = [e_d0, e_d1, e_ds0, e_ds1]
    (visit,) = pair_sums(guest, [(e_xs, lead, early - lead), e_ys, *e_d], [visit], 1024, narrow=True)
    visit, home = fence((visit, home))
    back = partner(visit)
    (home,) = pair_sums([x], [(e_s, ahead, early - ahead), e_x, e_y, e_xs, e_ys, *e_d], [home], 1024)
    (home,) = pair_sums([x], [c, c_s], [home], 768)
    c_x, c_y, home = fence((c_x, c_y, home))

    c_d0, c_d1 = corner(c_x, c_y)
    (home,) = pair_sums([x], [c_x, c_y, core(c_x), core(c_y)], [home], 768)
    c_d0, c_d1, back, home = fence((c_d0, c_d1, back, home))
    c_d = [c_d0, c_d1, core(c_d0), core(c_d1)]
    return tuple(pair_sums([x], c_d, [home], 768, back=back))


def gram_rows(left, right):
    return lax.dot_general(
        left, right, (((1,), (1,)), ((), ())), preferred_element_type=jnp.float32
    )


def apply_rows(hadam, right):
    return jnp.dot(hadam, right, preferred_element_type=jnp.float32)


def block_terms(lefts, rights):
    grams = [gram_rows(l, r) for l, r in zip(lefts, rights)]
    hadam_a = (grams[1] * grams[2]).astype(jnp.bfloat16)
    hadam_b = (grams[2] * grams[0]).astype(jnp.bfloat16)
    hadam_c = (grams[0] * grams[1]).astype(jnp.bfloat16)
    hadams = (hadam_a, hadam_b, hadam_c)
    return jnp.concatenate([apply_rows(h, r) for h, r in zip(hadams, rights)], axis=1)


def shards(factor_a, factor_b, factor_c):
    own_rows = factor_a.shape[0]
    length = factor_a.shape[1]
    block_j = (
        lax.all_gather(factor_a, "row", axis=0, tiled=True),
        lax.all_gather(factor_b, "row", axis=0, tiled=True),
        lax.all_gather(factor_c, "row", axis=0, tiled=True),
    )
    block_i = (
        lax.all_gather(factor_a, "col", axis=0, tiled=True),
        lax.all_gather(factor_b, "col", axis=0, tiled=True),
        lax.all_gather(factor_c, "col", axis=0, tiled=True),
    )
    lefts = [x for x in block_i]
    summed = lax.psum_scatter(
        block_terms(lefts, block_j).astype(jnp.bfloat16), "col", scatter_dimension=0, tiled=True
    ).astype(jnp.float32)
    cube_a = factor_a.astype(jnp.float32).reshape(own_rows, NMAT, NMAT)
    cube_b = factor_b.astype(jnp.float32).reshape(own_rows, NMAT, NMAT)
    cube_c = factor_c.astype(jnp.float32).reshape(own_rows, NMAT, NMAT)
    data_a = jnp.einsum("rjk,rki->rij", cube_b, cube_c).reshape(own_rows, length)
    data_b = jnp.einsum("rki,rij->rjk", cube_c, cube_a).reshape(own_rows, length)
    data_c = jnp.einsum("rij,rjk->rki", cube_a, cube_b).reshape(own_rows, length)
    grad_a = NMAT * (summed[:, :length] - data_a)
    grad_b = NMAT * (summed[:, length : 2 * length] - data_b)
    grad_c = NMAT * (summed[:, 2 * length :] - data_c)
    return (grad_a, grad_b, grad_c)


def solution(mesh):
    spec = P(("col", "row"), None)
    near = (mesh.shape["row"], mesh.shape["col"]) == (8, 4)
    return jax.shard_map(
        near_shards if near else shards, mesh=mesh, in_specs=(spec,) * 3, out_specs=(spec,) * 3, check_vma=False
    )
```

```python
import functools

import jax
import jax.numpy as jnp
from jax import lax
from jax.experimental import pallas as pl
from jax.experimental.pallas import tpu as pltpu
from jax.sharding import PartitionSpec as P

NMAT = 32
ROW_TILE = 256
LANES = 128
VMEM_BYTES = 63 * 1024 * 1024 + 512 * 1024


def trace_kernel(feat, x_ref, out_ref, left, right, prod):
    blocks = [slice(f * feat, (f + 1) * feat) for f in range(3)]
    for out, (l, r) in enumerate(((1, 2), (2, 0), (0, 1))):
        left[...] = x_ref[:, blocks[l]].astype(jnp.float32).T
        right[...] = x_ref[:, blocks[r]].astype(jnp.float32).T

        def rows(step, carry):
            base = step * 4
            sums = [None] * 4
            for k in range(NMAT):
                line = right[k * NMAT : (k + 1) * NMAT, :]
                for n in range(4):
                    term = left[pl.ds((base + n) * NMAT + k, 1), :] * line
                    sums[n] = term if k == 0 else sums[n] + term
            for n in range(4):
                prod[pl.ds(base + n, NMAT, stride=NMAT), :] = sums[n]
            return carry

        lax.fori_loop(0, NMAT // 4, rows, 0)
        out_ref[:, blocks[out]] = -prod[...].T


def trace_terms(x):
    rows, width = x.shape
    feat = width // 3
    spec = pl.BlockSpec((LANES, width), lambda i: (i, 0))
    return pl.pallas_call(
        functools.partial(trace_kernel, feat),
        grid=(rows // LANES,),
        in_specs=[spec],
        out_specs=spec,
        out_shape=jax.ShapeDtypeStruct((rows, width), jnp.float32),
        scratch_shapes=[pltpu.VMEM((feat, LANES), jnp.float32)] * 3,
        compiler_params=pltpu.CompilerParams(vmem_limit_bytes=VMEM_BYTES),
        cost_estimate=pl.CostEstimate(flops=rows, bytes_accessed=width, transcendentals=0),
    )(x)


def pair_kernel(feat, i_rows, spans, tile, n_sums, narrow, has_y, final, *refs):
    refs = list(refs)
    take = lambda n: [refs.pop(0) for _ in range(n)]
    tiles = sum(count for _, count in spans) // tile
    n_i = sum(i_rows) // ROW_TILE
    per = n_i // n_sums
    blocks = [slice(f * feat, (f + 1) * feat) for f in range(3)]
    i_refs, j_refs = take(len(i_rows)), take(len(spans))
    y_refs = take(n_sums) if has_y else []
    back_ref = take(1)[0] if final else None
    out_refs = take(3 if final else n_sums)
    ibuf, jbuf, acc, i_sem, j_sem, y_sem, o_sem = take(7)
    packed, b_sem = take(2) if narrow or final else (None, None)

    def block(i):
        return pl.ds(i * ROW_TILE, ROW_TILE)

    def fill(buf, sem, sources, ranges, t, size):
        low = 0
        for ref, (first, count) in zip(sources, ranges):
            a, b = max(low, t * size), min(low + count, (t + 1) * size)
            if a < b:
                src = ref.at[pl.ds(first + a - low, b - a)]
                pltpu.make_async_copy(src, buf.at[pl.ds(a, b - a)], sem.at[t]).start()
            low += count

    fill(jbuf, j_sem, j_refs, spans, 0, tile)
    for i in range(n_i):
        fill(ibuf, i_sem, i_refs, [(0, count) for count in i_rows], i, ROW_TILE)
        if has_y:
            pltpu.make_async_copy(y_refs[i // per].at[block(i % per)], acc.at[block(i)], y_sem.at[i]).start()
    for t in range(1, tiles):
        fill(jbuf, j_sem, j_refs, spans, t, tile)
    for i in range(n_i if final else 0):
        pltpu.make_async_copy(back_ref.at[block(i)], packed.at[block(i)], b_sem.at[i]).start()

    def wait(ref, sem):
        pltpu.make_async_copy(ref, ref, sem).wait()

    def over_tiles(t, carry):
        cols = pl.ds(pl.multiple_of(t * tile, tile), tile)
        wait(jbuf.at[cols], j_sem.at[t])

        def over_rows(i, inner):
            span = pl.ds(pl.multiple_of(i * ROW_TILE, ROW_TILE), ROW_TILE)

            @pl.when(t == 0)
            def _():
                wait(ibuf.at[span], i_sem.at[i])

            grams = [
                lax.dot_general(ibuf[span, b], jbuf[cols, b], (((1,), (1,)), ((), ())), preferred_element_type=jnp.float32)
                for b in blocks
            ]
            hadams = [(grams[(f + 1) % 3] * grams[(f + 2) % 3]).astype(jnp.bfloat16) for f in range(3)]

            @pl.when(t == 0)
            def _():
                if has_y:
                    wait(acc.at[span], y_sem.at[i])
                else:
                    acc[span, :] = jnp.zeros((ROW_TILE, 3 * feat), jnp.float32)

            for hadam, b in zip(hadams, blocks):
                acc[span, b] += jnp.dot(hadam, jbuf[cols, b], preferred_element_type=jnp.float32)

            @pl.when(t == tiles - 1)
            def _():
                if final:
                    wait(packed.at[span], b_sem.at[i])
                    acc[span, :] = NMAT * (acc[span, :] + packed[span, :].astype(jnp.float32))
                    for out, b in zip(out_refs, blocks):
                        pltpu.make_async_copy(acc.at[span, b], out.at[span], o_sem.at[i]).start()
                for n in range(0 if final else n_i):
                    @pl.when(i == n)
                    def _():
                        if narrow:
                            packed[block(n), :] = acc[block(n), :].astype(jnp.bfloat16)
                        src = (packed if narrow else acc).at[block(n)]
                        pltpu.make_async_copy(src, out_refs[n // per].at[block(n % per)], o_sem.at[n]).start()
            return inner

        return lax.fori_loop(0, n_i, over_rows, carry)

    lax.fori_loop(0, tiles, over_tiles, 0)
    for i in range(n_i):
        wait((packed if narrow else acc).at[block(i)], o_sem.at[i])


def pair_sums(lefts, rights, sums, tile, narrow=False, back=None):
    width = lefts[0].shape[1]
    feat = width // 3
    i_rows = [v.shape[0] for v in lefts]
    rows = sum(i_rows)
    rights = [r if isinstance(r, tuple) else (r, 0, r.shape[0]) for r in rights]
    spans = [(first, count) for _, first, count in rights]
    total = sum(count for _, count in spans)
    assert total % tile == 0 and rows % ROW_TILE == 0
    n_i = rows // ROW_TILE
    has_y, final = sums is not None, back is not None
    n_sums = len(sums) if has_y else 1
    any_spec = pl.BlockSpec(memory_space=pltpu.HBM)
    operands = [*lefts, *(r for r, _, _ in rights), *(sums or []), *([back] if final else [])]
    first_y = len(lefts) + len(rights)
    if final:
        outs = [jax.ShapeDtypeStruct((rows, feat), jnp.float32)] * 3
    else:
        outs = [jax.ShapeDtypeStruct((rows // n_sums, width), jnp.bfloat16 if narrow else jnp.float32)] * n_sums
    scratch = [
        pltpu.VMEM((rows, width), jnp.bfloat16),
        pltpu.VMEM((total, width), jnp.bfloat16),
        pltpu.VMEM((rows, width), jnp.float32),
        pltpu.SemaphoreType.DMA((n_i,)),
        pltpu.SemaphoreType.DMA((total // tile,)),
        pltpu.SemaphoreType.DMA((n_i,)),
        pltpu.SemaphoreType.DMA((n_i,)),
    ]
    if narrow or final:
        scratch += [pltpu.VMEM((rows, width), jnp.bfloat16), pltpu.SemaphoreType.DMA((n_i,))]
    return pl.pallas_call(
        functools.partial(pair_kernel, feat, i_rows, spans, tile, n_sums, narrow, has_y, final),
        in_specs=[any_spec] * len(operands),
        out_specs=[any_spec] * len(outs),
        out_shape=outs,
        scratch_shapes=scratch,
        input_output_aliases={first_y + n: n for n in range(n_sums)} if has_y and not narrow and not final else {},
        compiler_params=pltpu.CompilerParams(vmem_limit_bytes=VMEM_BYTES),
        cost_estimate=pl.CostEstimate(flops=rows, bytes_accessed=width, transcendentals=0),
    )(*operands)


def cut_kernel(mid, parts, x_ref, y_ref, low_ref, high_ref, low, high, sem):
    size = mid // parts
    spans = [pl.ds(n * size, size) for n in range(parts)]
    moves = []
    for n, span in enumerate(spans):
        moves.append((y_ref.at[span], low.at[span], low_ref.at[span], n))
        moves.append((x_ref.at[pl.ds(mid + n * size, size)], high.at[span], high_ref.at[span], parts + n))
    first = [pltpu.make_async_copy(src, buf, sem.at[0, n]) for src, buf, _, n in moves]
    last = [pltpu.make_async_copy(buf, dst, sem.at[1, n]) for _, buf, dst, n in moves]
    for copy in first:
        copy.start()
    for copy, then in zip(first, last):
        copy.wait()
        then.start()
    for copy in last:
        copy.wait()


def cut(from_x, from_y):
    rows, width = from_x.shape
    mid, parts = rows // 2, 2
    spec = pl.BlockSpec(memory_space=pltpu.HBM)
    return pl.pallas_call(
        functools.partial(cut_kernel, mid, parts),
        in_specs=[spec] * 2,
        out_specs=[spec] * 2,
        out_shape=[jax.ShapeDtypeStruct((mid, width), from_x.dtype)] * 2,
        scratch_shapes=[pltpu.VMEM((mid, width), from_x.dtype)] * 2 + [pltpu.SemaphoreType.DMA((2, 2 * parts))],
        cost_estimate=pl.CostEstimate(flops=0, bytes_accessed=rows * width, transcendentals=0),
    )(from_x, from_y)


def join_kernel(parts, a_ref, b_ref, c_ref, out_ref, low_ref, high_ref, buf, sem):
    rows, feat = a_ref.shape
    size = rows // parts
    spans = [pl.ds(n * size, size) for n in range(parts)]
    loads = [
        [
            pltpu.make_async_copy(ref.at[span], buf.at[span, pl.ds(f * feat, feat)], sem.at[f, n])
            for f, ref in enumerate((a_ref, b_ref, c_ref))
        ]
        for n, span in enumerate(spans)
    ]
    stores = [pltpu.make_async_copy(buf.at[span], out_ref.at[span], sem.at[3, n]) for n, span in enumerate(spans)]
    for copies in loads:
        for copy in copies:
            copy.start()
    for copies, store in zip(loads, stores):
        for copy in copies:
            copy.wait()
        store.start()
    low = low_ref.shape[0]
    stores.append(pltpu.make_async_copy(buf.at[pl.ds(0, low)], low_ref, sem.at[4, 0]))
    stores.append(pltpu.make_async_copy(buf.at[pl.ds(low, rows - low)], high_ref, sem.at[4, 1]))
    for store in stores[-2:]:
        store.start()
    for store in stores:
        store.wait()


def side_by_side(a, b, c, low):
    rows, feat = a.shape
    parts = 4
    spec = pl.BlockSpec(memory_space=pltpu.HBM)
    outs = [jax.ShapeDtypeStruct((n, 3 * feat), a.dtype) for n in (rows, low, rows - low)]
    return pl.pallas_call(
        functools.partial(join_kernel, parts),
        in_specs=[spec] * 3,
        out_specs=[spec] * 3,
        out_shape=outs,
        scratch_shapes=[pltpu.VMEM(outs[0].shape, a.dtype), pltpu.SemaphoreType.DMA((5, parts))],
        cost_estimate=pl.CostEstimate(flops=rows, bytes_accessed=feat, transcendentals=0),
    )(a, b, c)


def pick_kernel(rows, parts, flag_ref, *refs):
    count = len(rows)
    out_ref, buf, sem = refs[2 * count :]
    spans = []
    for n, size in enumerate(rows):
        for m in range(parts):
            spans.append((n, m * size // parts, sum(rows[:n]) + m * size // parts, size // parts))

    def load(sources):
        for k, (n, src, dst, size) in enumerate(spans):
            pltpu.make_async_copy(sources[n].at[pl.ds(src, size)], buf.at[pl.ds(dst, size)], sem.at[0, k]).start()

    pl.when(flag_ref[0] == 1)(lambda: load(refs[:count]))
    pl.when(flag_ref[0] != 1)(lambda: load(refs[count : 2 * count]))
    stores = []
    for k, (_, _, dst, size) in enumerate(spans):
        part = buf.at[pl.ds(dst, size)]
        pltpu.make_async_copy(part, part, sem.at[0, k]).wait()
        stores.append(pltpu.make_async_copy(part, out_ref.at[pl.ds(dst, size)], sem.at[1, k]))
        stores[-1].start()
    for store in stores:
        store.wait()


def pick(flag, ones, others):
    rows, width = [v.shape[0] for v in ones], ones[0].shape[1]
    parts = 2
    spec = pl.BlockSpec(memory_space=pltpu.HBM)
    out = jax.ShapeDtypeStruct((sum(rows), width), ones[0].dtype)
    return pl.pallas_call(
        functools.partial(pick_kernel, rows, parts),
        in_specs=[pl.BlockSpec(memory_space=pltpu.SMEM)] + [spec] * (2 * len(ones)),
        out_specs=spec,
        out_shape=out,
        scratch_shapes=[pltpu.VMEM(out.shape, out.dtype), pltpu.SemaphoreType.DMA((2, parts * len(ones)))],
        cost_estimate=pl.CostEstimate(flops=out.shape[0], bytes_accessed=width, transcendentals=0),
    )(flag, *ones, *others)


def near_shards(factor_a, factor_b, factor_c):
    rows = factor_a.shape[0]
    early = rows * 5 // 8
    x, part_a, part_c = side_by_side(factor_a, factor_b, factor_c, early)
    row = lax.axis_index("row")
    inner = ((row >= 2) & (row < 6)).astype(jnp.int32).reshape(1)
    fence = lax.optimization_barrier

    def move(axis, pairs):
        return lambda v: lax.ppermute(v, axis, pairs)

    core = move("row", [(r, r ^ 1) for r in range(8)])
    partner = move("row", [(r, r ^ 2) for r in range(8)])
    across = move("row", [(2, 4), (3, 5), (4, 2), (5, 3)])
    outward = move("row", [(2, 0), (3, 1), (4, 6), (5, 7)])
    along_x = move("col", [(c, c ^ 1) for c in range(4)])
    along_y = move("col", [(c, c ^ 2) for c in range(4)])

    def corner(from_x, from_y):
        low, high = cut(from_x, from_y)
        return along_x(low), along_y(high)

    x_x, x_y, x_s = along_x(x), along_y(x), core(x)
    guest_a, far_a = partner(part_a), across(part_a)
    home = trace_terms(x)
    (home,) = pair_sums([x], [x, x_s], [home], 1024)
    guest_a, far_a, part_c, home = fence((guest_a, far_a, part_c, home))

    guest_c, far_c = partner(part_c), across(part_c)
    x_x, x_y, guest_c, far_c, home = fence((x_x, x_y, guest_c, far_c, home))

    guest = [guest_a, guest_c]
    out_a, next_b = outward(far_a), across(guest_a)
    x_d0, x_d1 = corner(x_x, x_y)
    x_xs, x_ys = fence((core(x_x), core(x_y)))
    (visit,) = pair_sums(guest, [x, x_s, x_x, x_y, x_xs, x_ys], None, 1024)
    x_d0, x_d1, out_a, next_b, visit = fence((x_d0, x_d1, out_a, next_b, visit))

    e = pick(inner, [next_b], [out_a])
    e_x, e_y = along_x(e), along_y(e)
    x_ds0, x_ds1, e_s = fence((core(x_d0), core(x_d1), core(e)))
    x_d = [x_d0, x_d1, x_ds0, x_ds1]
    out_c0, next_c = outward(far_c), across(guest_c)
    ahead = rows - early
    (home,) = pair_sums([x], [x_x, x_y, x_xs, x_ys, *x_d, e, (e_s, 0, ahead)], [home], 1792)
    e_x, e_y, out_c0, next_c, home = fence((e_x, e_y, out_c0, next_c, home))

    e_d0, e_d1 = corner(e_x, e_y)
    out_c1 = outward(next_c)
    e_xs, e_ys = fence((core(e_x), core(e_y)))
    lead = 3 * rows - 4 * early
    (visit,) = pair_sums(guest, [*x_d, e, e_s, e_x, e_y, (e_xs, 0, lead)], [visit], 1280)
    e_d0, e_d1, out_c1, visit = fence((e_d0, e_d1, out_c1, visit))

    c = pick(inner, [far_c, next_c], [out_c0, out_c1])
    c, e_ds0, e_ds1 = fence((c, core(e_d0), core(e_d1)))
    c_x, c_y, c_s = along_x(c), along_y(c), core(c)
    e_d = [e_d0, e_d1, e_ds0, e_ds1]
    (visit,) = pair_sums(guest, [(e_xs, lead, early - lead), e_ys, *e_d], [visit], 1024, narrow=True)
    visit, home = fence((visit, home))
    back = partner(visit)
    (home,) = pair_sums([x], [(e_s, ahead, early - ahead), e_x, e_y, e_xs, e_ys, *e_d], [home], 1024)
    (home,) = pair_sums([x], [c, c_s], [home], 768)
    c_x, c_y, home = fence((c_x, c_y, home))

    c_d0, c_d1 = corner(c_x, c_y)
    (home,) = pair_sums([x], [c_x, c_y, core(c_x), core(c_y)], [home], 768)
    c_d0, c_d1, back, home = fence((c_d0, c_d1, back, home))
    c_d = [c_d0, c_d1, core(c_d0), core(c_d1)]
    return tuple(pair_sums([x], c_d, [home], 768, back=back))


def gram_rows(left, right):
    return lax.dot_general(
        left, right, (((1,), (1,)), ((), ())), preferred_element_type=jnp.float32
    )


def apply_rows(hadam, right):
    return jnp.dot(hadam, right, preferred_element_type=jnp.float32)


def block_terms(lefts, rights):
    grams = [gram_rows(l, r) for l, r in zip(lefts, rights)]
    hadam_a = (grams[1] * grams[2]).astype(jnp.bfloat16)
    hadam_b = (grams[2] * grams[0]).astype(jnp.bfloat16)
    hadam_c = (grams[0] * grams[1]).astype(jnp.bfloat16)
    hadams = (hadam_a, hadam_b, hadam_c)
    return jnp.concatenate([apply_rows(h, r) for h, r in zip(hadams, rights)], axis=1)


def shards(factor_a, factor_b, factor_c):
    own_rows = factor_a.shape[0]
    length = factor_a.shape[1]
    block_j = (
        lax.all_gather(factor_a, "row", axis=0, tiled=True),
        lax.all_gather(factor_b, "row", axis=0, tiled=True),
        lax.all_gather(factor_c, "row", axis=0, tiled=True),
    )
    block_i = (
        lax.all_gather(factor_a, "col", axis=0, tiled=True),
        lax.all_gather(factor_b, "col", axis=0, tiled=True),
        lax.all_gather(factor_c, "col", axis=0, tiled=True),
    )
    lefts = [x for x in block_i]
    summed = lax.psum_scatter(
        block_terms(lefts, block_j).astype(jnp.bfloat16), "col", scatter_dimension=0, tiled=True
    ).astype(jnp.float32)
    cube_a = factor_a.astype(jnp.float32).reshape(own_rows, NMAT, NMAT)
    cube_b = factor_b.astype(jnp.float32).reshape(own_rows, NMAT, NMAT)
    cube_c = factor_c.astype(jnp.float32).reshape(own_rows, NMAT, NMAT)
    data_a = jnp.einsum("rjk,rki->rij", cube_b, cube_c).reshape(own_rows, length)
    data_b = jnp.einsum("rki,rij->rjk", cube_c, cube_a).reshape(own_rows, length)
    data_c = jnp.einsum("rij,rjk->rki", cube_a, cube_b).reshape(own_rows, length)
    grad_a = NMAT * (summed[:, :length] - data_a)
    grad_b = NMAT * (summed[:, length : 2 * length] - data_b)
    grad_c = NMAT * (summed[:, 2 * length :] - data_c)
    return (grad_a, grad_b, grad_c)


def solution(mesh):
    spec = P(("col", "row"), None)
    near = (mesh.shape["row"], mesh.shape["col"]) == (8, 4)
    return jax.shard_map(
        near_shards if near else shards, mesh=mesh, in_specs=(spec,) * 3, out_specs=(spec,) * 3, check_vma=False
    )
```
